32 devices in a mesh: stretch: 16 (over z, x, core), chan: 2 (over y).
Axes of the slice: x: 2, y: 2, z: 4, core: 2. Of those that a mesh axis runs over, the one named last changes fastest.
Arguments:
- tokens: bfloat16 [8192, 4096], P('stretch', 'chan'), may hold values from -6 to 6
- in_weight: bfloat16 [4096, 3, 4096], P('stretch', None, 'chan'), may hold values from -0.09375 to 0.09375
- short_weight: bfloat16 [7, 3, 4096], P(None, None, 'chan'), may hold values from -2.390625 to 2.390625
- medium_filter: bfloat16 [128, 256], P(None, 'chan'), may hold values from -1 to 1
- seq_lengths: int32 [8], replicated, may hold values from 1 to 2048, 8192 in all
- stretch_slot: int32 [16], replicated, may hold values from 0 to 15, as said below
Outputs:
- gated_output: bfloat16 [8192, 4096], P('stretch', 'chan')
The draws below stay inside these ranges and needn't reach their ends.
Inputs may be any that keep to these rules, and one draw needn't show every extreme that they name: stretch_slot is a permutation; stretches 2k and 2k + 1 are held at indices 2k and 2k + 1 in some order, so stretch_slot[c] - stretch_slot[c - 1] is one of -1, 1, 2, 3.
All inputs are finite; a program needn't handle non-finite values.
Results may differ from the reference program's by a relative error of at most 0.007.
Values may be sent and summed in bfloat16 or wider, within the bound.
No kernel may reach another device: no remote copies, remote signals or barrier semaphores. Data moves between devices by JAX's collectives and lax.ppermute only.
A program may use at most 128 MiB of HBM per device.

```python
import math
import jax
import jax.numpy as jnp
import numpy as np
from jax import lax

D = 4096
HC = 4096
KS = 7
KM = 128
NSEQ = 8
STRETCHES = 16
TOKENS = 8192
FILTERS = 256


def draw_stretch_slot(key, part):
    coin_flips = jax.random.randint(jax.random.fold_in(key, 7), (STRETCHES // 2,), 0, 2, dtype=jnp.int32)
    stretch_order = jnp.arange(STRETCHES, dtype=jnp.int32)
    return stretch_order ^ jnp.repeat(coin_flips, 2)


def draw_medium_filter(key, part):
    key_noise = jax.random.fold_in(key, 11)
    key_rate = jax.random.fold_in(key, 12)
    raw_values = jax.random.normal(key_noise, (KM, FILTERS), jnp.float32)
    decay_rates = jnp.exp(jax.random.uniform(key_rate, (FILTERS,), jnp.float32, math.log(1.0 / 400.0), math.log(1.0 / 24.0)))
    lag_steps = jnp.arange(KM, dtype=jnp.float32)[:, None]
    return jnp.clip(0.12 * raw_values * jnp.exp(-lag_steps * decay_rates[None, :]), -1.0, 1.0).astype(jnp.bfloat16)


def block_scale(own_key, extent, split, least, high):
    gain, own = 1.0, jax.random.fold_in(own_key, 6)
    for position, blocks in split:
        steps = jnp.exp(jax.random.uniform(jax.random.fold_in(own, position), (blocks,), jnp.float32, least / len(split), high / len(split)))
        gain = gain * jnp.repeat(steps, extent[position] // blocks).reshape([-1 if axis == position else 1 for axis in range(len(extent))])
    return gain


def split_up(number_of, total, bound, skew):
    weights = [(1 << 20) // math.isqrt(grade ** skew) + 1 for grade in range(2, number_of + 1)]
    spare, given = total - bound - (number_of - 1), [1] * (number_of - 1)
    while spare > 0:
        candidates = [i for i in range(number_of - 1) if given[i] < bound]
        pool, budget = sum([weights[i] for i in candidates]), spare
        for i in candidates:
            more = min(bound - given[i], max(1, budget * weights[i] // pool), spare)
            given[i] = given[i] + more
            spare = spare - more
    return np.array([bound] + given)


def uneven_parts(rng, number_of, total, limit, lean):
    if number_of == 2:
        one = jax.random.randint(rng, (), max(1, total - limit), min(limit, total - 1) + 1)
        return jnp.stack([one, total - one])
    tallies = jnp.asarray(split_up(number_of, total, limit, lean), jnp.int32)
    twos = (number_of - 1) // 2
    donor, taker = tallies[1:1 + 2 * twos:2], tallies[2:2 + 2 * twos:2]
    slack = jnp.minimum(donor - 1, limit - taker)
    passed = jax.random.randint(jax.random.fold_in(rng, 1), (twos,), 0, 1 << 20) % (slack + 1)
    tallies = tallies.at[1:1 + 2 * twos:2].set(donor - passed).at[2:2 + 2 * twos:2].set(taker + passed)
    return tallies[jax.random.permutation(jax.random.fold_in(rng, 2), number_of)]


def centred(key, extent, width, bound, cuts=(), held_as=jnp.bfloat16):
    loudness = block_scale(key, extent, cuts, -0.22, 0.18) if cuts else 1.0
    result = jax.random.normal(key, extent, jnp.float32) * width * loudness
    return jnp.minimum(jnp.maximum(result, -bound), bound).astype(held_as)


def setup_inputs(seed: int = 0) -> dict:
    key_of = jax.random.split(jax.random.key(seed), 7)
    tokens = centred(key_of[0], (TOKENS, D), 1.0, 6.0, ((0, 16), (1, 2)))
    in_weight = centred(key_of[1], (D, 3, HC), D ** -0.5, 0.09375, ((0, 16), (2, 2)))
    short_weight = centred(key_of[2], (KS, 3, HC), 0.4, 2.390625, ((2, 2),))
    medium_filter = draw_medium_filter(jax.random.fold_in(key_of[6], 71), 0)
    seq_lengths = uneven_parts(key_of[4], NSEQ, TOKENS, TOKENS // 4, 2).astype(jnp.int32)
    stretch_slot = draw_stretch_slot(jax.random.fold_in(key_of[6], 71), 0)
    return dict(tokens=tokens, in_weight=in_weight, short_weight=short_weight, medium_filter=medium_filter, seq_lengths=seq_lengths, stretch_slot=stretch_slot)


def in_sequence(places, seq_lengths):
    lengths = seq_lengths.astype(jnp.int32)
    seq_ends = jnp.cumsum(lengths).astype(jnp.int32)
    starts = seq_ends - lengths
    inside = (places[:, None] >= starts[None, :]) & (places[:, None] < seq_ends[None, :])
    return jnp.sum(jnp.where(inside, places[:, None] - starts[None, :], 0), axis=1).astype(jnp.int32)


def short_conv(extended, weights, positions):
    tap_count = weights.shape[0]
    row_count = extended.shape[0] - tap_count + 1
    shape_tail = (1,) * (extended.ndim - 1)
    running = jnp.zeros((row_count,) + extended.shape[1:], jnp.float32)
    for lag_index in range(tap_count):
        start_row = tap_count - 1 - lag_index
        window = extended[start_row:start_row + row_count].astype(jnp.float32)
        allowed = (positions >= lag_index).reshape((row_count,) + shape_tail)
        running = running + jnp.where(allowed, window * weights[lag_index].astype(jnp.float32), 0.0)
    return running


def reference(tokens, in_weight, short_weight, medium_filter, seq_lengths, stretch_slot):
    stretch_count = stretch_slot.shape[0]
    row_count = tokens.shape[0] // stretch_count
    feature_count = tokens.shape[1]
    chan_width = in_weight.shape[2]
    tap_count = short_weight.shape[0]
    span_len = medium_filter.shape[0]
    tail_reach = span_len + tap_count - 2
    packed_rows = tokens.reshape(stretch_count, row_count, feature_count)[stretch_slot.astype(jnp.int32)]
    packed_rows = packed_rows.reshape(-1, feature_count)
    projected = jnp.dot(packed_rows, in_weight.reshape(feature_count, -1), preferred_element_type=jnp.float32)
    projected = projected.astype(jnp.bfloat16).reshape(-1, 3, chan_width)
    padded = jnp.concatenate([jnp.zeros((tail_reach, 3, chan_width), jnp.bfloat16), projected], axis=0)
    per_channel = jnp.repeat(medium_filter, chan_width // medium_filter.shape[1], axis=1)

    def one_stretch(stretch_id):
        first_place = stretch_id * row_count
        window = lax.dynamic_slice_in_dim(padded, first_place, row_count + tail_reach, 0)
        places = first_place - (span_len - 1) + jnp.arange(row_count + span_len - 1, dtype=jnp.int32)
        positions = in_sequence(places, seq_lengths)
        short_out = short_conv(window, short_weight, positions)
        mixed_in = (short_out[:, 0] * short_out[:, 2]).astype(jnp.bfloat16)
        own_positions = positions[span_len - 1:]

        def add_lag(lag_index, running):
            shifted = lax.dynamic_slice_in_dim(mixed_in, span_len - 1 - lag_index, row_count, 0).astype(jnp.float32)
            weights = lax.dynamic_slice_in_dim(per_channel, lag_index, 1, 0).astype(jnp.float32)
            allowed = (own_positions >= lag_index)[:, None]
            return running + jnp.where(allowed, shifted * weights, 0.0)

        medium = lax.fori_loop(0, span_len, add_lag, jnp.zeros((row_count, chan_width), jnp.float32))
        return (short_out[span_len - 1:, 1] * medium).astype(jnp.bfloat16)

    outputs = lax.map(one_stretch, jnp.arange(stretch_count, dtype=jnp.int32))
    placed = jnp.zeros_like(outputs).at[stretch_slot.astype(jnp.int32)].set(outputs)
    return placed.reshape(-1, chan_width)
```

```python
import functools

import jax
import jax.numpy as jnp
from jax import lax
from jax.experimental import pallas as pl
from jax.experimental.pallas import tpu as pltpu
from jax.sharding import PartitionSpec as P

ROW_TILE = 256
CHAN_TILE = 256
LANES = 128


def in_sequence(places, seq_lengths):
    seq_ends = jnp.cumsum(seq_lengths)
    starts = seq_ends - seq_lengths
    inside = (places[:, None] >= starts[None, :]) & (places[:, None] < seq_ends[None, :])
    return jnp.sum(jnp.where(inside, places[:, None] - starts[None, :], 0), axis=1)


def block_kernel(x_ref, w_ref, sw_ref, fr_ref, pos_ref, out_ref, proj, mix, band):
    i = pl.program_id(1)
    taps = sw_ref.shape[1]
    rows, chans = out_ref.shape
    span = band.shape[0] // fr_ref.shape[0]
    groups = fr_ref.shape[0]
    per_lanes = groups * LANES // chans
    width = LANES // per_lanes

    @pl.when(i == 0)
    def _():
        proj[:, :8, :] = jnp.zeros((3, 8, chans), jnp.float32)
        mix[:span, :] = jnp.zeros((span, chans), mix.dtype)
        for g in range(groups):
            row = jnp.broadcast_to(fr_ref[g : g + 1, :], (span, 2 * span))
            band[g * span : (g + 1) * span, :] = pltpu.roll(
                row, 0, 1, stride=1, stride_axis=0
            ).astype(band.dtype)

    for s in range(3):
        weight = w_ref[:, s].reshape(x_ref.shape[1], chans)
        acc = jnp.dot(x_ref[...], weight, preferred_element_type=jnp.float32)
        proj[s, 8:, :] = acc.astype(jnp.bfloat16).astype(jnp.float32)

    def short(s, start, size, lanes, allowed):
        total = proj[s, 8 + start : 8 + start + size, lanes] * sw_ref[s, 0:1, lanes]
        for j in range(1, taps):
            window = proj[s, 8 + start - j : 8 + start - j + size, lanes]
            total = total + jnp.where(allowed[j], window * sw_ref[s, j : j + 1, lanes], 0.0)
        return total

    step = 64
    for r in range(rows // step):
        pos = pos_ref[r * step : (r + 1) * step, :]
        allowed = [pos >= j for j in range(taps)]
        for h in range(chans // LANES):
            lanes = slice(h * LANES, (h + 1) * LANES)
            mixed = short(0, r * step, step, lanes, allowed) * short(2, r * step, step, lanes, allowed)
            mix[span + r * step : span + (r + 1) * step, lanes] = mixed.astype(mix.dtype)

    @pl.when(i > 0)
    def _():
        lag = (
            lax.broadcasted_iota(jnp.int32, (span, 2 * span), 0)
            + span
            - lax.broadcasted_iota(jnp.int32, (span, 2 * span), 1)
        )
        lane_group = lax.broadcasted_iota(jnp.int32, (span, LANES), 1) // width
        for b in range(rows // span):
            pos = pos_ref[b * span : (b + 1) * span, :]
            limit = jnp.concatenate([pos] * (2 * span // LANES), axis=1)
            keep = jnp.where(lag <= limit, 1.0, 0.0).astype(band.dtype)
            allowed = [pos >= j for j in range(taps)]
            for h in range(chans // LANES):
                lanes = slice(h * LANES, (h + 1) * LANES)
                some = band[h * per_lanes * span : (h + 1) * per_lanes * span, :]
                some = some.reshape(per_lanes, span, 2 * span) * keep[None]
                full = jnp.dot(
                    some.reshape(per_lanes * span, 2 * span),
                    mix[b * span : (b + 2) * span, lanes],
                    preferred_element_type=jnp.float32,
                )
                medium = full[:span]
                for g in range(1, per_lanes):
                    medium = jnp.where(lane_group == g, full[g * span : (g + 1) * span], medium)
                gate = short(1, b * span, span, lanes, allowed)
                out_ref[b * span : (b + 1) * span, lanes] = (gate * medium).astype(out_ref.dtype)

    proj[:, :8, :] = proj[:, rows : rows + 8, :]
    mix[:span, :] = mix[rows : rows + span, :]


def block(x, w, sw, fr, pos, first_chan, span):
    total, features = x.shape
    pieces, _, depth, chans = w.shape
    taps = sw.shape[1]
    per_tile = CHAN_TILE * fr.shape[0] // sw.shape[2]
    first = first_chan // CHAN_TILE
    grid = (chans // CHAN_TILE, total // ROW_TILE)
    return pl.pallas_call(
        block_kernel,
        grid=grid,
        in_specs=[
            pl.BlockSpec((ROW_TILE, features), lambda j, i: (i, 0)),
            pl.BlockSpec((pieces, 3, depth, CHAN_TILE), lambda j, i: (0, 0, 0, j)),
            pl.BlockSpec((3, taps, CHAN_TILE), lambda j, i: (0, 0, first + j)),
            pl.BlockSpec((per_tile, 2 * span), lambda j, i: (first + j, 0)),
            pl.BlockSpec((ROW_TILE, LANES), lambda j, i: (i, 0)),
        ],
        out_specs=pl.BlockSpec((ROW_TILE, CHAN_TILE), lambda j, i: (jnp.maximum(i - 1, 0), j)),
        out_shape=jax.ShapeDtypeStruct((total - ROW_TILE, chans), jnp.bfloat16),
        scratch_shapes=[
            pltpu.VMEM((3, 8 + ROW_TILE, CHAN_TILE), jnp.float32),
            pltpu.VMEM((span + ROW_TILE, CHAN_TILE), jnp.bfloat16),
            pltpu.VMEM((per_tile * span, 2 * span), jnp.bfloat16),
        ],
        compiler_params=pltpu.CompilerParams(vmem_limit_bytes=40 * 1024 * 1024),
        cost_estimate=pl.CostEstimate(
            flops=2 * total * features * 3 * chans + 2 * total * chans // CHAN_TILE * per_tile * span * 256,
            bytes_accessed=2 * (total * features * grid[0] + 3 * features * chans + total * chans),
            transcendentals=0,
        ),
    )(x, w, sw, fr, pos)


def parameters(short_weight, medium_filter):
    sw = jnp.transpose(short_weight, (1, 0, 2)).astype(jnp.float32)
    span = medium_filter.shape[0]
    fr = jnp.pad(jnp.flip(medium_filter, axis=0).T.astype(jnp.float32), ((0, 0), (1, span - 1)))
    return sw, fr


def chunks_of(chans):
    large = 2 * CHAN_TILE
    widths = [large] * max(0, chans // large - 1)
    rest = chans - sum(widths)
    return widths + [CHAN_TILE] * (rest // CHAN_TILE)


def per_device(tokens, in_weight, short_weight, medium_filter, seq_lengths, stretch_slot):
    row_count = tokens.shape[0]
    chans = in_weight.shape[2]
    span, taps = medium_filter.shape[0], short_weight.shape[0]
    device = lax.axis_index("stretch")
    devices = lax.axis_size("stretch")
    order = jnp.arange(devices, dtype=jnp.int32)
    stretch_id = jnp.sum(jnp.where(stretch_slot == device, order, 0))

    local = jnp.transpose(in_weight, (1, 0, 2))
    gathered, begin = [], 0
    for width in chunks_of(chans):
        part = local[:, :, begin : begin + width]
        gathered.append((begin, lax.all_gather(part, "stretch", axis=0, tiled=False)))
        begin += width

    reach = -(-(span + taps - 1) // 16) * 16
    tail = tokens[row_count - reach :]
    sibling = lax.ppermute(tail, "stretch", [(i, i ^ 1) for i in range(devices)])
    second = stretch_id % 2 == 1
    last = jnp.where(second, tail, sibling)
    before = lax.ppermute(last, "stretch", [(i, i + 2) for i in range(devices - 2)])
    halo = jnp.where(second, sibling, before)
    mine = jnp.concatenate([halo, tokens], axis=0)
    x = lax.all_gather(mine, "chan", axis=1, tiled=True) if lax.axis_size("chan") != 2 else None
    if x is None:
        other = lax.ppermute(mine, "chan", [(0, 1), (1, 0)])
        low = lax.axis_index("chan") == 0
        x = jnp.concatenate([jnp.where(low, mine, other), jnp.where(low, other, mine)], axis=1)
    x = jnp.pad(x, ((ROW_TILE - reach, 0), (0, 0)))

    places = stretch_id * row_count - ROW_TILE + jnp.arange(ROW_TILE + row_count, dtype=jnp.int32)
    pos = jnp.broadcast_to(in_sequence(places, seq_lengths)[:, None], (ROW_TILE + row_count, LANES))
    sw, fr = parameters(short_weight, medium_filter)
    outs = [block(x, w, sw, fr, pos, begin, span) for begin, w in gathered]
    return jnp.concatenate(outs, axis=1)


def solution(mesh):
    return jax.shard_map(
        per_device,
        mesh=mesh,
        in_specs=(
            P("stretch", "chan"),
            P("stretch", None, "chan"),
            P(None, None, "chan"),
            P(None, "chan"),
            P(),
            P(),
        ),
        out_specs=P("stretch", "chan"),
        check_vma=False,
    )
```

```python
import jax
import jax.numpy as jnp
from jax import lax
from jax.experimental import pallas as pl
from jax.experimental.pallas import tpu as pltpu
from jax.sharding import PartitionSpec as P

ROW_TILE = 256
CHAN_TILE = 256
LANES = 128


def in_sequence(places, seq_lengths):
    seq_ends = jnp.cumsum(seq_lengths)
    starts = seq_ends - seq_lengths
    inside = (places[:, None] >= starts[None, :]) & (places[:, None] < seq_ends[None, :])
    return jnp.sum(jnp.where(inside, places[:, None] - starts[None, :], 0), axis=1)


def block_kernel(at_ref, x_ref, *refs):
    *w_refs, sw_ref, fr_ref, pos_ref, out_ref, proj, mix, band = refs
    total, rows, chans = x_ref.shape[1], out_ref.shape[1], out_ref.shape[2]
    halo = total - rows
    taps = sw_ref.shape[1]
    groups = fr_ref.shape[0]
    span = band.shape[0] // groups
    per_lanes = groups * LANES // chans
    width = LANES // per_lanes
    depth = w_refs[0].shape[2]

    @pl.when(pl.program_id(1) == 0)
    def _():
        proj[:, :8, :] = jnp.zeros((3, 8, chans), jnp.float32)
        for g in range(groups):
            row = jnp.broadcast_to(fr_ref[g : g + 1, :], (span, 2 * span))
            band[g * span : (g + 1) * span, :] = pltpu.roll(
                row, 0, 1, stride=1, stride_axis=0
            ).astype(band.dtype)

    units = [(w, k) for w in w_refs for k in range(w.shape[0])]
    align = LANES if depth % LANES == 0 else depth
    starts = [pl.multiple_of(at_ref[u], align) for u in range(len(units))]
    edges = [0, halo] + list(range(halo + ROW_TILE, total + 1, ROW_TILE))
    for low, high in zip(edges[:-1], edges[1:]):
        if depth % LANES == 0:
            x = jnp.concatenate([x_ref[0, low:high, pl.ds(at, depth)] for at in starts], axis=1)
        else:
            x = x_ref[0, low:high, :]
        for s in range(3):
            weight = jnp.concatenate([w[k, s] for w, k in units], axis=0)
            acc = jnp.dot(x, weight, preferred_element_type=jnp.float32)
            proj[s, 8 + low : 8 + high, :] = acc.astype(jnp.bfloat16).astype(jnp.float32)

    def short(s, start, size, lanes, allowed):
        running = proj[s, 8 + start : 8 + start + size, lanes] * sw_ref[s, 0:1, lanes]
        for j in range(1, taps):
            window = proj[s, 8 + start - j : 8 + start - j + size, lanes]
            running = running + jnp.where(allowed[j], window * sw_ref[s, j : j + 1, lanes], 0.0)
        return running

    step = 64
    for r in range(halo - span, total, step):
        pos = pos_ref[0, r : r + step, :]
        allowed = [pos >= j for j in range(taps)]
        for h in range(chans // LANES):
            lanes = slice(h * LANES, (h + 1) * LANES)
            mixed = short(0, r, step, lanes, allowed) * short(2, r, step, lanes, allowed)
            mix[r : r + step, lanes] = mixed.astype(mix.dtype)

    lag = (
        lax.broadcasted_iota(jnp.int32, (span, 2 * span), 0)
        + span
        - lax.broadcasted_iota(jnp.int32, (span, 2 * span), 1)
    )
    lane_group = lax.broadcasted_iota(jnp.int32, (span, LANES), 1) // width
    for b in range(rows // span):
        first = halo + b * span
        pos = pos_ref[0, first : first + span, :]
        limit = jnp.concatenate([pos] * (2 * span // LANES), axis=1)
        keep = jnp.where(lag <= limit, 1.0, 0.0).astype(band.dtype)
        allowed = [pos >= j for j in range(taps)]
        for h in range(chans // LANES):
            lanes = slice(h * LANES, (h + 1) * LANES)
            some = band[h * per_lanes * span : (h + 1) * per_lanes * span, :]
            some = some.reshape(per_lanes, span, 2 * span) * keep[None]
            full = jnp.dot(
                some.reshape(per_lanes * span, 2 * span),
                mix[first - span : first + span, lanes],
                preferred_element_type=jnp.float32,
            )
            medium = full[:span]
            for g in range(1, per_lanes):
                medium = jnp.where(lane_group == g, full[g * span : (g + 1) * span], medium)
            gate = short(1, first, span, lanes, allowed)
            out_ref[0, b * span : (b + 1) * span, lanes] = (gate * medium).astype(out_ref.dtype)


def block(at, x, weights, sw, fr, pos, span, rows):
    runs, total, features = x.shape
    depth, chans = weights[0].shape[2:]
    taps = sw.shape[1]
    tile = min(CHAN_TILE, chans)
    per_tile = tile * fr.shape[0] // chans
    grid = (chans // tile, runs)
    return pl.pallas_call(
        block_kernel,
        grid_spec=pltpu.PrefetchScalarGridSpec(
            num_scalar_prefetch=1,
            grid=grid,
            in_specs=[pl.BlockSpec((1, total, features), lambda j, i, at: (i, 0, 0))]
            + [pl.BlockSpec((w.shape[0], 3, depth, tile), lambda j, i, at: (0, 0, 0, j)) for w in weights]
            + [
                pl.BlockSpec((3, taps, tile), lambda j, i, at: (0, 0, j)),
                pl.BlockSpec((per_tile, 2 * span), lambda j, i, at: (j, 0)),
                pl.BlockSpec((1, total, LANES), lambda j, i, at: (i, 0, 0)),
            ],
            out_specs=pl.BlockSpec((1, rows, tile), lambda j, i, at: (i, 0, j)),
            scratch_shapes=[
                pltpu.VMEM((3, 8 + total, tile), jnp.float32),
                pltpu.VMEM((total, tile), jnp.bfloat16),
                pltpu.VMEM((per_tile * span, 2 * span), jnp.bfloat16),
            ],
        ),
        out_shape=jax.ShapeDtypeStruct((runs, rows, chans), jnp.bfloat16),
        compiler_params=pltpu.CompilerParams(vmem_limit_bytes=56 * 1024 * 1024),
        cost_estimate=pl.CostEstimate(
            flops=2 * runs * total * features * 3 * chans + 2 * runs * rows * (chans // tile) * per_tile * span * 256,
            bytes_accessed=2 * (runs * total * features * grid[0] + 3 * features * chans + runs * rows * chans),
            transcendentals=0,
        ),
    )(at, x, *weights, sw, fr, pos)


def parameters(short_weight, medium_filter):
    sw = jnp.transpose(short_weight, (1, 0, 2)).astype(jnp.float32)
    span = medium_filter.shape[0]
    fr = jnp.pad(jnp.flip(medium_filter, axis=0).T.astype(jnp.float32), ((0, 0), (1, span - 1)))
    return sw, fr


def flip(array, bit):
    return lax.ppermute(array, "stretch", [(i, i ^ bit) for i in range(lax.axis_size("stretch"))])


def across(array):
    return lax.ppermute(array, "chan", [(0, 1), (1, 0)])


def rows_before(tokens, stretch_id, reach):
    tail = tokens[tokens.shape[0] - reach :]
    sibling = flip(tail, 1)
    second = stretch_id % 2 == 1
    pairs = [(i, i + 2) for i in range(lax.axis_size("stretch") - 2)]
    before = lax.ppermute(jnp.where(second, tail, sibling), "stretch", pairs)
    return jnp.where(second, sibling, before)


def whole_rows(halo, halo_other, rows, rows_other, low):
    left = jnp.concatenate([jnp.where(low, halo, halo_other), jnp.where(low, rows, rows_other)], axis=0)
    right = jnp.concatenate([jnp.where(low, halo_other, halo), jnp.where(low, rows_other, rows)], axis=0)
    return jnp.concatenate([left, right], axis=1)


def tied(value, other):
    return lax.optimization_barrier((value, other))


def per_device(tokens, in_weight, short_weight, medium_filter, seq_lengths, stretch_slot):
    row_count = tokens.shape[0]
    depth, _, chans = in_weight.shape
    span, taps = medium_filter.shape[0], short_weight.shape[0]
    me = lax.axis_index("stretch")
    devices = lax.axis_size("stretch")
    order = jnp.arange(devices, dtype=jnp.int32)
    reach = -(-(span + taps - 1) // 16) * 16
    sw, fr = parameters(short_weight, medium_filter)
    local = jnp.transpose(in_weight, (1, 0, 2))

    def stretch_at(device):
        return jnp.sum(jnp.where(stretch_slot == device, order, 0))

    def positions(device):
        places = stretch_at(device) * row_count - reach + jnp.arange(reach + row_count, dtype=jnp.int32)
        return jnp.broadcast_to(in_sequence(places, seq_lengths)[:, None], (reach + row_count, LANES))

    if devices != 16 or lax.axis_size("chan") != 2:
        weight = lax.all_gather(local, "stretch", axis=0, tiled=False)
        rows = jnp.concatenate([rows_before(tokens, stretch_at(me), reach), tokens], axis=0)
        x = lax.all_gather(rows, "chan", axis=1, tiled=True)
        out = block(order * depth, x[None], [weight], sw, fr, positions(me)[None], span, row_count)
        return out[0]

    low = lax.axis_index("chan") == 0
    kind = (me >> 2) & 1
    half = chans // 2
    own_begin, other_begin = kind * half, (1 - kind) * half

    peer_rows = flip(tokens, 4)
    rows_other = across(tokens)
    halo = rows_before(tokens, stretch_at(me), reach)
    halo_other = across(halo)
    peer_halo = flip(halo, 4)

    widths = [CHAN_TILE] * (half // CHAN_TILE)
    begins = [sum(widths[:c]) for c in range(len(widths))]
    arrived = []
    for c, (begin, width) in enumerate(zip(begins, widths)):
        here = local
        if c == 1:
            here, peer_rows = tied(here, peer_rows)
        if c >= 2:
            here, arrived[c - 2] = tied(here, arrived[c - 2])
        own = lax.dynamic_slice_in_dim(here, own_begin + begin, width, 2)
        other = lax.dynamic_slice_in_dim(here, other_begin + begin, width, 2)
        arrived.append([own, flip(other, 4), flip(own, 8), flip(other, 12)])

    peer_rows_other = across(peer_rows)
    peer_halo_other = across(peer_halo)
    x = jnp.stack(
        [
            whole_rows(halo, halo_other, tokens, rows_other, low),
            whole_rows(peer_halo, peer_halo_other, peer_rows, peer_rows_other, low),
        ]
    )
    pos = jnp.stack([positions(me), positions(me ^ 4)])
    at = jnp.stack([me ^ (4 * k + q) for q in (0, 2, 1, 3) for k in range(4)]) * depth
    own_sw = lax.dynamic_slice_in_dim(sw, own_begin, half, 2)
    own_fr = lax.dynamic_slice_in_dim(fr, own_begin * fr.shape[0] // chans, fr.shape[0] // 2, 0)

    mine, theirs = [], []
    for c, (begin, width) in enumerate(zip(begins, widths)):
        line = jnp.stack(arrived[c])
        beside = flip(line, 2)
        weights = [line, beside, flip(line, 1), flip(beside, 1)]
        groups = fr.shape[0] * width // chans
        first_group = begin * fr.shape[0] // chans
        out = block(
            at,
            x,
            weights,
            own_sw[:, :, begin : begin + width],
            own_fr[first_group : first_group + groups],
            pos,
            span,
            row_count,
        )
        mine.append(out[0])
        theirs.append(flip(out[1], 4))
    mine, theirs = jnp.concatenate(mine, axis=1), jnp.concatenate(theirs, axis=1)
    even = kind == 0
    return jnp.concatenate([jnp.where(even, mine, theirs), jnp.where(even, theirs, mine)], axis=1)


def solution(mesh):
    return jax.shard_map(
        per_device,
        mesh=mesh,
        in_specs=(
            P("stretch", "chan"),
            P("stretch", None, "chan"),
            P(None, None, "chan"),
            P(None, "chan"),
            P(),
            P(),
        ),
        out_specs=P("stretch", "chan"),
        check_vma=False,
    )
```

```python
import functools

import jax
import jax.numpy as jnp
from jax import lax
from jax.experimental import pallas as pl
from jax.experimental.pallas import tpu as pltpu
from jax.sharding import PartitionSpec as P

ROW_TILE = 256
CHAN_TILE = 256
LANES = 128
WIDTHS = [256, 256, 256, 256]


def in_sequence(places, seq_lengths):
    seq_ends = jnp.cumsum(seq_lengths)
    starts = seq_ends - seq_lengths
    inside = (places[:, None] >= starts[None, :]) & (places[:, None] < seq_ends[None, :])
    return jnp.sum(jnp.where(inside, places[:, None] - starts[None, :], 0), axis=1)


def block_kernel(runs, halves, at_ref, w_ref, sw_ref, fr_ref, pos_ref, *refs):
    row_refs, halo_refs = refs[: runs * halves], refs[runs * halves : (runs + 1) * halves]
    out_refs = refs[(runs + 1) * halves : (runs + 1) * halves + runs]
    x_ref, sems, proj, mix, band = refs[(runs + 1) * halves + runs :]
    total, features = x_ref.shape[1:]
    rows, chans = out_refs[0].shape
    halo = total - rows
    taps = sw_ref.shape[1]
    groups = fr_ref.shape[0]
    span = band.shape[0] // groups
    per_lanes = groups * LANES // chans
    width = LANES // per_lanes
    outer, inner, _, depth, _ = w_ref.shape
    units = [(q, k) for q in range(outer) for k in range(inner)]
    tile, run = pl.program_id(0), pl.program_id(1)

    def copies(r):
        for h in range(halves):
            piece = features // halves
            where = pl.ds(pl.multiple_of(at_ref[len(units) + h], piece), piece)
            yield pltpu.make_async_copy(
                halo_refs[h].at[r], x_ref.at[r, pl.ds(0, halo), where], sems.at[r, 2 * h]
            )
            yield pltpu.make_async_copy(
                row_refs[r * halves + h], x_ref.at[r, pl.ds(halo, rows), where], sems.at[r, 2 * h + 1]
            )

    @pl.when((tile == 0) & (run == 0))
    def _():
        for r in range(runs):
            for copy in copies(r):
                copy.start()

    @pl.when(run == 0)
    def _():
        proj[:, :, :8, :] = jnp.zeros((3, chans // LANES, 8, LANES), jnp.float32)
        for g in range(groups):
            row = jnp.broadcast_to(fr_ref[g : g + 1, :], (span, 2 * span))
            band[g * span : (g + 1) * span, :] = pltpu.roll(
                row, 0, 1, stride=1, stride_axis=0
            ).astype(band.dtype)

    for r in range(runs):

        @pl.when((tile == 0) & (run == r))
        def _():
            for copy in copies(r):
                copy.wait()

    edges = [0, halo] + list(range(halo + ROW_TILE, total + 1, ROW_TILE))
    for low, high in zip(edges[:-1], edges[1:]):
        if depth % LANES == 0:
            starts = [pl.multiple_of(at_ref[u], LANES) for u in range(len(units))]
            x = jnp.concatenate([x_ref[run, low:high, pl.ds(at, depth)] for at in starts], axis=1)
        else:
            x = x_ref[run, low:high, :]
        for s in range(3):
            weight = jnp.concatenate([w_ref[q, k, s] for q, k in units], axis=0)
            acc = jnp.dot(x, weight, preferred_element_type=jnp.float32)
            acc = acc.astype(jnp.bfloat16).astype(jnp.float32)
            for h in range(chans // LANES):
                proj[s, h, 8 + low : 8 + high, :] = acc[:, h * LANES : (h + 1) * LANES]

    def short(s, start, size, h, allowed):
        lanes = slice(h * LANES, (h + 1) * LANES)
        running = proj[s, h, 8 + start : 8 + start + size, :] * sw_ref[s, 0:1, lanes]
        for j in range(1, taps):
            window = proj[s, h, 8 + start - j : 8 + start - j + size, :]
            running = running + jnp.where(allowed[j], window * sw_ref[s, j : j + 1, lanes], 0.0)
        return running

    step = 64
    for r in range(halo - span, total, step):
        pos = pos_ref[0, r : r + step, :]
        allowed = [pos >= j for j in range(taps)]
        for h in range(chans // LANES):
            mixed = short(0, r, step, h, allowed) * short(2, r, step, h, allowed)
            mix[r : r + step, h * LANES : (h + 1) * LANES] = mixed.astype(mix.dtype)

    lag = (
        lax.broadcasted_iota(jnp.int32, (span, 2 * span), 0)
        + span
        - lax.broadcasted_iota(jnp.int32, (span, 2 * span), 1)
    )
    lane_group = lax.broadcasted_iota(jnp.int32, (span, LANES), 1) // width
    for b in range(rows // span):
        first = halo + b * span
        pos = pos_ref[0, first : first + span, :]
        limit = jnp.concatenate([pos] * (2 * span // LANES), axis=1)
        keep = jnp.where(lag <= limit, 1.0, 0.0).astype(band.dtype)
        allowed = [pos >= j for j in range(taps)]
        for h in range(chans // LANES):
            lanes = slice(h * LANES, (h + 1) * LANES)
            some = band[h * per_lanes * span : (h + 1) * per_lanes * span, :]
            some = some.reshape(per_lanes, span, 2 * span) * keep[None]
            full = jnp.dot(
                some.reshape(per_lanes * span, 2 * span),
                mix[first - span : first + span, lanes],
                preferred_element_type=jnp.float32,
            )
            medium = full[:span]
            for g in range(1, per_lanes):
                medium = jnp.where(lane_group == g, full[g * span : (g + 1) * span], medium)
            gated = (short(1, first, span, h, allowed) * medium).astype(out_refs[0].dtype)
            for r in range(runs):

                @pl.when(run == r)
                def _():
                    out_refs[r][b * span : (b + 1) * span, lanes] = gated


def block(at, rows, halos, weight, sw, fr, pos, span):
    runs, halves = len(rows), len(halos)
    row_count, features = rows[0][0].shape[0], rows[0][0].shape[1] * halves
    total = halos[0].shape[1] + row_count
    outer, inner, _, depth, chans = weight.shape
    taps = sw.shape[1]
    tile = CHAN_TILE if chans % CHAN_TILE == 0 else LANES
    per_tile = tile * fr.shape[0] // chans
    grid = (chans // tile, runs)
    anywhere = pl.BlockSpec(memory_space=pl.ANY)
    return pl.pallas_call(
        functools.partial(block_kernel, runs, halves),
        grid_spec=pltpu.PrefetchScalarGridSpec(
            num_scalar_prefetch=1,
            grid=grid,
            in_specs=[
                pl.BlockSpec((outer, inner, 3, depth, tile), lambda j, i, at: (0, 0, 0, 0, j)),
                pl.BlockSpec((3, taps, tile), lambda j, i, at: (0, 0, j)),
                pl.BlockSpec((per_tile, 2 * span), lambda j, i, at: (j, 0)),
                pl.BlockSpec((1, total, LANES), lambda j, i, at: (i, 0, 0)),
            ]
            + [anywhere] * (runs * halves + halves),
            out_specs=[pl.BlockSpec((row_count, tile), lambda j, i, at: (0, j))] * runs,
            scratch_shapes=[
                pltpu.VMEM((runs, total, features), jnp.bfloat16),
                pltpu.SemaphoreType.DMA((runs, 2 * halves)),
                pltpu.VMEM((3, tile // LANES, 8 + total, LANES), jnp.float32),
                pltpu.VMEM((total, tile), jnp.bfloat16),
                pltpu.VMEM((per_tile * span, 2 * span), jnp.bfloat16),
            ],
        ),
        out_shape=[jax.ShapeDtypeStruct((row_count, chans), jnp.bfloat16)] * runs,
        compiler_params=pltpu.CompilerParams(vmem_limit_bytes=56 * 1024 * 1024),
        cost_estimate=pl.CostEstimate(
            flops=4 * runs * total * features * 3 * chans,
            bytes_accessed=2 * (runs * total * features + 3 * features * chans + runs * row_count * chans),
            transcendentals=0,
        ),
    )(at, weight, sw, fr, pos, *[half for run in rows for half in run], *halos)


def parameters(short_weight, medium_filter):
    sw = jnp.transpose(short_weight, (1, 0, 2)).astype(jnp.float32)
    span = medium_filter.shape[0]
    fr = jnp.pad(jnp.flip(medium_filter, axis=0).T.astype(jnp.float32), ((0, 0), (1, span - 1)))
    return sw, fr


def flip(array, bit):
    return lax.ppermute(array, "stretch", [(i, i ^ bit) for i in range(lax.axis_size("stretch"))])


def across(array):
    return lax.ppermute(array, "chan", [(0, 1), (1, 0)])


def rows_before(tokens, stretch_id, reach):
    tail = tokens[tokens.shape[0] - reach :]
    sibling = flip(tail, 1)
    second = stretch_id % 2 == 1
    pairs = [(i, i + 2) for i in range(lax.axis_size("stretch") - 2)]
    before = lax.ppermute(jnp.where(second, tail, sibling), "stretch", pairs)
    return jnp.where(second, sibling, before)


def nothing(array):
    return (array[(0,) * array.ndim].astype(jnp.float32) * 0.0).astype(jnp.int32)


def per_device(tokens, in_weight, short_weight, medium_filter, seq_lengths, stretch_slot):
    row_count, piece = tokens.shape
    depth, _, chans = in_weight.shape
    span, taps = medium_filter.shape[0], short_weight.shape[0]
    me = lax.axis_index("stretch")
    devices = lax.axis_size("stretch")
    order = jnp.arange(devices, dtype=jnp.int32)
    reach = -(-(span + taps - 1) // 16) * 16
    sw, fr = parameters(short_weight, medium_filter)
    local = jnp.transpose(in_weight, (1, 0, 2))

    def stretch_at(device):
        return jnp.sum(jnp.where(stretch_slot == device, order, 0))

    def positions(device):
        places = stretch_at(device) * row_count - reach + jnp.arange(reach + row_count, dtype=jnp.int32)
        return jnp.broadcast_to(in_sequence(places, seq_lengths)[:, None], (reach + row_count, LANES))

    if devices != 16 or lax.axis_size("chan") != 2:
        weight = lax.all_gather(local, "stretch", axis=0, tiled=False)
        halo = rows_before(tokens, stretch_at(me), reach)
        halo = lax.all_gather(halo, "chan", axis=1, tiled=True)
        rows = lax.all_gather(tokens, "chan", axis=1, tiled=True)
        at = jnp.concatenate([order * depth, jnp.zeros(1, jnp.int32)])
        return block(at, [[rows]], [halo[None]], weight[:, None], sw, fr, positions(me)[None], span)[0]

    side = lax.axis_index("chan")
    kind = (me >> 2) & 1
    half = chans // 2
    own_begin, other_begin = kind * half, (1 - kind) * half
    widths = WIDTHS if sum(WIDTHS) == half else [half]
    begins = [sum(widths[:c]) for c in range(len(widths))]

    halo = rows_before(tokens, stretch_at(me), reach)
    peer_rows = flip(tokens, 4)
    rows_other = across(tokens)
    peer_rows_other = across(peer_rows)
    peer_halo = flip(halo, 4)
    halos = jnp.stack([halo, peer_halo])
    halos_other = across(halos)
    after = {1: [peer_rows], 2: [rows_other, peer_halo], 3: [peer_rows_other]}

    planes = [[4 * z + q for q in range(4)] for z in range(devices // 4)]
    arrived, gathered = [], []
    for c, (begin, width) in enumerate(zip(begins, widths)):
        units = [lax.dynamic_slice_in_dim(local, own_begin + begin, width, 2)]
        for k in (1, 2, 3):
            start = (own_begin if k == 2 else other_begin) + begin
            if c > 0:
                start = start + sum(nothing(first) for first in [arrived[c - 1][k]] + after.get(c, []))
            units.append(flip(lax.dynamic_slice_in_dim(local, start, width, 2), 4 * k))
        arrived.append(units)
        whole = lax.all_gather(jnp.stack(units), "stretch", axis=0, tiled=False, axis_index_groups=planes)
        gathered.append(whole)
        after.setdefault(c + 2, []).append(whole)

    pos = jnp.stack([positions(me), positions(me ^ 4)])
    at = jnp.concatenate(
        [
            jnp.stack([((me ^ (4 * k)) // 4 * 4 + q) * depth for q in range(4) for k in range(4)]),
            jnp.stack([side * piece, (1 - side) * piece]),
        ]
    )
    own_sw = lax.dynamic_slice_in_dim(sw, own_begin, half, 2)
    own_fr = lax.dynamic_slice_in_dim(fr, own_begin * fr.shape[0] // chans, fr.shape[0] // 2, 0)

    mine, theirs = [], []
    for c, (begin, width) in enumerate(zip(begins, widths)):
        groups = fr.shape[0] * width // chans
        first_group = begin * fr.shape[0] // chans
        out, peer_out = block(
            at,
            [[tokens, rows_other], [peer_rows, peer_rows_other]],
            [halos, halos_other],
            gathered[c],
            own_sw[:, :, begin : begin + width],
            own_fr[first_group : first_group + groups],
            pos,
            span,
        )
        mine.append(out)
        theirs.append(flip(peer_out, 4))
    mine, theirs = jnp.concatenate(mine, axis=1), jnp.concatenate(theirs, axis=1)
    even = kind == 0
    return jnp.concatenate([jnp.where(even, mine, theirs), jnp.where(even, theirs, mine)], axis=1)


def solution(mesh):
    return jax.shard_map(
        per_device,
        mesh=mesh,
        in_specs=(
            P("stretch", "chan"),
            P("stretch", None, "chan"),
            P(None, None, "chan"),
            P(None, "chan"),
            P(),
            P(),
        ),
        out_specs=P("stretch", "chan"),
        check_vma=False,
    )
```

```python
import functools

import jax
import jax.numpy as jnp
from jax import lax
from jax.experimental import pallas as pl
from jax.experimental.pallas import tpu as pltpu
from jax.sharding import PartitionSpec as P

ROW_TILE = 256
CHAN_TILE = 256
LANES = 128
WIDTHS = [256, 256, 256, 256]


def in_sequence(places, seq_lengths):
    seq_ends = jnp.cumsum(seq_lengths)
    starts = seq_ends - seq_lengths
    inside = (places[:, None] >= starts[None, :]) & (places[:, None] < seq_ends[None, :])
    return jnp.sum(jnp.where(inside, places[:, None] - starts[None, :], 0), axis=1)


def block_kernel(runs, halves, parts, at_ref, *refs):
    w_refs, (sw_ref, fr_ref, pos_ref), refs = refs[:parts], refs[parts : parts + 3], refs[parts + 3 :]
    row_refs, halo_refs = refs[: runs * halves], refs[runs * halves : (runs + 1) * halves]
    out_refs = refs[(runs + 1) * halves : (runs + 1) * halves + runs]
    x_ref, sems, proj, mix, band, done = refs[(runs + 1) * halves + runs :]
    total, features = x_ref.shape[1:]
    rows, chans = out_refs[0].shape
    halo = total - rows
    taps = sw_ref.shape[1]
    groups = fr_ref.shape[0]
    span = band.shape[0] // groups
    per_lanes = groups * LANES // chans
    width = LANES // per_lanes
    depth = w_refs[0].shape[3]
    units = [(w, q, k) for w in w_refs for q in range(w.shape[0]) for k in range(w.shape[1])]
    tile, run = pl.program_id(0), pl.program_id(1)

    def copies(r):
        for h in range(halves):
            piece = features // halves
            where = pl.ds(pl.multiple_of(at_ref[len(units) + h], piece), piece)
            yield pltpu.make_async_copy(
                halo_refs[h].at[r], x_ref.at[r, pl.ds(0, halo), where], sems.at[r, 2 * h]
            )
            yield pltpu.make_async_copy(
                row_refs[r * halves + h], x_ref.at[r, pl.ds(halo, rows), where], sems.at[r, 2 * h + 1]
            )

    @pl.when((tile == 0) & (run == 0))
    def _():
        for r in range(runs):
            for copy in copies(r):
                copy.start()

    @pl.when(run == 0)
    def _():
        proj[:, :, :8, :] = jnp.zeros((3, chans // LANES, 8, LANES), jnp.float32)
        for g in range(groups):
            row = jnp.broadcast_to(fr_ref[g : g + 1, :], (span, 2 * span))
            band[g * span : (g + 1) * span, :] = pltpu.roll(
                row, 0, 1, stride=1, stride_axis=0
            ).astype(band.dtype)

    for r in range(runs):

        @pl.when((tile == 0) & (run == r))
        def _():
            for copy in copies(r):
                copy.wait()

    edges = [0, halo] + list(range(halo + ROW_TILE, total + 1, ROW_TILE))
    for low, high in zip(edges[:-1], edges[1:]):
        if depth % LANES == 0:
            starts = [pl.multiple_of(at_ref[u], LANES) for u in range(len(units))]
            x = jnp.concatenate([x_ref[run, low:high, pl.ds(at, depth)] for at in starts], axis=1)
        else:
            x = x_ref[run, low:high, :]
        for streams in [(0, 1, 2)] if chans == LANES else [(0,), (1,), (2,)]:
            weight = jnp.concatenate(
                [jnp.concatenate([w[q, k, s] for w, q, k in units], axis=0) for s in streams], axis=1
            )
            acc = jnp.dot(x, weight, preferred_element_type=jnp.float32)
            acc = acc.astype(jnp.bfloat16).astype(jnp.float32)
            for n, s in enumerate(streams):
                for h in range(chans // LANES):
                    lane = n * chans + h * LANES
                    proj[s, h, 8 + low : 8 + high, :] = acc[:, lane : lane + LANES]

    def short(s, start, size, h, allowed):
        lanes = slice(h * LANES, (h + 1) * LANES)
        running = proj[s, h, 8 + start : 8 + start + size, :] * sw_ref[s, 0:1, lanes]
        for j in range(1, taps):
            window = proj[s, h, 8 + start - j : 8 + start - j + size, :]
            running = running + jnp.where(allowed[j], window * sw_ref[s, j : j + 1, lanes], 0.0)
        return running

    step = 64
    for r in range(halo - span, total, step):
        pos = pos_ref[0, r : r + step, :]
        allowed = [pos >= j for j in range(taps)]
        for h in range(chans // LANES):
            mixed = short(0, r, step, h, allowed) * short(2, r, step, h, allowed)
            mix[r : r + step, h * LANES : (h + 1) * LANES] = mixed.astype(mix.dtype)

    lag = (
        lax.broadcasted_iota(jnp.int32, (span, 2 * span), 0)
        + span
        - lax.broadcasted_iota(jnp.int32, (span, 2 * span), 1)
    )
    lane_group = lax.broadcasted_iota(jnp.int32, (span, LANES), 1) // width
    for b in range(rows // span):
        first = halo + b * span
        pos = pos_ref[0, first : first + span, :]
        limit = jnp.concatenate([pos] * (2 * span // LANES), axis=1)
        keep = jnp.where(lag <= limit, 1.0, 0.0).astype(band.dtype)
        allowed = [pos >= j for j in range(taps)]
        for h in range(chans // LANES):
            lanes = slice(h * LANES, (h + 1) * LANES)
            some = band[h * per_lanes * span : (h + 1) * per_lanes * span, :]
            some = some.reshape(per_lanes, span, 2 * span) * keep[None]
            full = jnp.dot(
                some.reshape(per_lanes * span, 2 * span),
                mix[first - span : first + span, lanes],
                preferred_element_type=jnp.float32,
            )
            medium = full[:span]
            for g in range(1, per_lanes):
                medium = jnp.where(lane_group == g, full[g * span : (g + 1) * span], medium)
            gated = short(1, first, span, h, allowed) * medium
            done[b * span : (b + 1) * span, lanes] = gated.astype(done.dtype)

    for r in range(runs):

        @pl.when(run == r)
        def _():
            out_refs[r][...] = done[...]


def block(at, rows, halos, weights, sw, fr, pos, span, chans):
    runs, halves = len(rows), len(halos)
    row_count, features = rows[0][0].shape[0], rows[0][0].shape[1] * halves
    total = halos[0].shape[1] + row_count
    taps = sw.shape[1]
    tile = CHAN_TILE if all(n % CHAN_TILE == 0 for n in [chans] + [first for first, _ in weights]) else LANES
    per_tile = tile * fr.shape[0] // chans
    grid = (chans // tile, runs)
    anywhere = pl.BlockSpec(memory_space=pl.ANY)

    def weight_spec(first, w):
        return pl.BlockSpec(w.shape[:4] + (tile,), lambda j, i, at: (0, 0, 0, 0, first // tile + j))

    return pl.pallas_call(
        functools.partial(block_kernel, runs, halves, len(weights)),
        grid_spec=pltpu.PrefetchScalarGridSpec(
            num_scalar_prefetch=1,
            grid=grid,
            in_specs=[weight_spec(first, w) for first, w in weights]
            + [
                pl.BlockSpec((3, taps, tile), lambda j, i, at: (0, 0, j)),
                pl.BlockSpec((per_tile, 2 * span), lambda j, i, at: (j, 0)),
                pl.BlockSpec((1, total, LANES), lambda j, i, at: (i, 0, 0)),
            ]
            + [anywhere] * (runs * halves + halves),
            out_specs=[pl.BlockSpec((row_count, tile), lambda j, i, at: (0, j))] * runs,
            scratch_shapes=[
                pltpu.VMEM((runs, total, features), jnp.bfloat16),
                pltpu.SemaphoreType.DMA((runs, 2 * halves)),
                pltpu.VMEM((3, tile // LANES, 8 + total, LANES), jnp.float32),
                pltpu.VMEM((total, tile), jnp.bfloat16),
                pltpu.VMEM((per_tile * span, 2 * span), jnp.bfloat16),
                pltpu.VMEM((row_count, tile), jnp.bfloat16),
            ],
        ),
        out_shape=[jax.ShapeDtypeStruct((row_count, chans), jnp.bfloat16)] * runs,
        compiler_params=pltpu.CompilerParams(vmem_limit_bytes=56 * 1024 * 1024),
        cost_estimate=pl.CostEstimate(
            flops=4 * runs * total * features * 3 * chans,
            bytes_accessed=2 * (runs * total * features + 3 * features * chans + runs * row_count * chans),
            transcendentals=0,
        ),
    )(at, *[w for _, w in weights], sw, fr, pos, *[half for run in rows for half in run], *halos)


def parameters(short_weight, medium_filter):
    sw = jnp.transpose(short_weight, (1, 0, 2)).astype(jnp.float32)
    span = medium_filter.shape[0]
    fr = jnp.pad(jnp.flip(medium_filter, axis=0).T.astype(jnp.float32), ((0, 0), (1, span - 1)))
    return sw, fr


def flip(array, bit):
    return lax.ppermute(array, "stretch", [(i, i ^ bit) for i in range(lax.axis_size("stretch"))])


def across(array):
    return lax.ppermute(array, "chan", [(0, 1), (1, 0)])


def rows_before(tokens, stretch_id, reach):
    tail = tokens[tokens.shape[0] - reach :]
    sibling = flip(tail, 1)
    second = stretch_id % 2 == 1
    pairs = [(i, i + 2) for i in range(lax.axis_size("stretch") - 2)]
    before = lax.ppermute(jnp.where(second, tail, sibling), "stretch", pairs)
    return jnp.where(second, sibling, before)


def nothing(array):
    return (array[(0,) * array.ndim].astype(jnp.float32) * 0.0).astype(jnp.int32)


def per_device(tokens, in_weight, short_weight, medium_filter, seq_lengths, stretch_slot):
    row_count, piece = tokens.shape
    depth, _, chans = in_weight.shape
    span, taps = medium_filter.shape[0], short_weight.shape[0]
    me = lax.axis_index("stretch")
    devices = lax.axis_size("stretch")
    order = jnp.arange(devices, dtype=jnp.int32)
    reach = -(-(span + taps - 1) // 16) * 16
    sw, fr = parameters(short_weight, medium_filter)
    local = jnp.transpose(in_weight, (1, 0, 2))

    def stretch_at(device):
        return jnp.sum(jnp.where(stretch_slot == device, order, 0))

    def positions(device):
        places = stretch_at(device) * row_count - reach + jnp.arange(reach + row_count, dtype=jnp.int32)
        return jnp.broadcast_to(in_sequence(places, seq_lengths)[:, None], (reach + row_count, LANES))

    if devices != 16 or lax.axis_size("chan") != 2:
        weight = lax.all_gather(local, "stretch", axis=0, tiled=False)
        halo = rows_before(tokens, stretch_at(me), reach)
        halo = lax.all_gather(halo, "chan", axis=1, tiled=True)
        rows = lax.all_gather(tokens, "chan", axis=1, tiled=True)
        at = jnp.concatenate([order * depth, jnp.zeros(1, jnp.int32)])
        return block(at, [[rows]], [halo[None]], [(0, weight[:, None])], sw, fr, positions(me)[None], span, chans)[0]

    side = lax.axis_index("chan")
    kind = (me >> 2) & 1
    half = chans // 2
    own_begin, other_begin = kind * half, (1 - kind) * half
    widths = WIDTHS if sum(WIDTHS) == half else [half]
    begins = [sum(widths[:c]) for c in range(len(widths))]

    halo = rows_before(tokens, stretch_at(me), reach)
    peer_rows = flip(tokens, 4)
    rows_other = across(tokens)
    peer_rows_other = across(peer_rows)
    peer_halo = flip(halo, 4)
    halos = jnp.stack([halo, peer_halo])
    halos_other = across(halos)
    after = {0: [peer_rows, rows_other, halo], 1: [peer_halo, peer_rows_other], 2: [halos_other]}

    planes = [[4 * z + q for q in range(4)] for z in range(devices // 4)]

    def spread(array):
        return lax.all_gather(array, "stretch", axis=0, tiled=False, axis_index_groups=planes)

    own = lax.dynamic_slice_in_dim(local, own_begin, half, 2)
    peers = [
        flip(lax.dynamic_slice_in_dim(local, other_begin + begin, width, 2), 4) for begin, width in zip(begins, widths)
    ]
    for c, peer in enumerate(peers[1:]):
        after[c] = after.get(c, []) + [peer]
    gathered, stack = [spread(own[None])], None
    for c, (begin, width) in enumerate(zip(begins, widths)):
        mine = own[:, :, begin : begin + width]
        peer = peers[c]
        pair = jnp.stack([mine, peer])
        if c > 0:
            pair = pair + nothing(stack).astype(jnp.bfloat16)
        stack = jnp.concatenate([peer[None], flip(pair, 8)])
        waits = sum(nothing(array) for array in after.get(c, []) + [gathered[-1]])
        stack = stack + waits.astype(jnp.bfloat16)
        gathered.append(spread(stack))

    pos = jnp.stack([positions(me), positions(me ^ 4)])
    at = jnp.concatenate(
        [
            jnp.stack([(me // 4 * 4 + q) * depth for q in range(4)]),
            jnp.stack([((me ^ (4 * k)) // 4 * 4 + q) * depth for q in range(4) for k in (1, 2, 3)]),
            jnp.stack([side * piece, (1 - side) * piece]),
        ]
    )
    own_sw = lax.dynamic_slice_in_dim(sw, own_begin, half, 2)
    own_fr = lax.dynamic_slice_in_dim(fr, own_begin * fr.shape[0] // chans, fr.shape[0] // 2, 0)

    mine, theirs = [], []
    for c, (begin, width) in enumerate(zip(begins, widths)):
        groups = fr.shape[0] * width // chans
        first_group = begin * fr.shape[0] // chans
        out, peer_out = block(
            at,
            [[tokens, rows_other], [peer_rows, peer_rows_other]],
            [halos, halos_other],
            [(begin, gathered[0]), (0, gathered[c + 1])],
            own_sw[:, :, begin : begin + width],
            own_fr[first_group : first_group + groups],
            pos,
            span,
            width,
        )
        mine.append(out)
        theirs.append(flip(peer_out, 4))
    mine, theirs = jnp.concatenate(mine, axis=1), jnp.concatenate(theirs, axis=1)
    even = kind == 0
    return jnp.concatenate([jnp.where(even, mine, theirs), jnp.where(even, theirs, mine)], axis=1)


def solution(mesh):
    return jax.shard_map(
        per_device,
        mesh=mesh,
        in_specs=(
            P("stretch", "chan"),
            P("stretch", None, "chan"),
            P(None, None, "chan"),
            P(None, "chan"),
            P(),
            P(),
        ),
        out_specs=P("stretch", "chan"),
        check_vma=False,
    )
```

```python
import functools

import jax
import jax.numpy as jnp
from jax import lax
from jax.experimental import pallas as pl
from jax.experimental.pallas import tpu as pltpu
from jax.sharding import PartitionSpec as P

ROW_TILE = 256
CHAN_TILE = 256
LANES = 128
WIDTHS = [256, 256, 256, 256]


def in_sequence(places, seq_lengths):
    seq_ends = jnp.cumsum(seq_lengths)
    starts = seq_ends - seq_lengths
    inside = (places[:, None] >= starts[None, :]) & (places[:, None] < seq_ends[None, :])
    return jnp.sum(jnp.where(inside, places[:, None] - starts[None, :], 0), axis=1)


def block_kernel(runs, halves, parts, at_ref, *refs):
    w_refs, (sw_ref, fr_ref, pos_ref), refs = refs[:parts], refs[parts : parts + 3], refs[parts + 3 :]
    row_refs, halo_refs = refs[: runs * halves], refs[runs * halves : (runs + 1) * halves]
    out_refs = refs[(runs + 1) * halves : (runs + 1) * halves + runs]
    x_ref, sems, proj, mix, band, done = refs[(runs + 1) * halves + runs :]
    total, features = x_ref.shape[1:]
    rows, chans = out_refs[0].shape
    halo = total - rows
    taps = sw_ref.shape[1]
    groups = fr_ref.shape[0]
    span = band.shape[0] // groups
    per_lanes = groups * LANES // chans
    width = LANES // per_lanes
    depth = w_refs[0].shape[3]
    units = [(w, q, k) for w in w_refs for q in range(w.shape[0]) for k in range(w.shape[1])]
    tile, run = pl.program_id(0), pl.program_id(1)

    def copies(r):
        for h in range(halves):
            piece = features // halves
            where = pl.ds(pl.multiple_of(at_ref[len(units) + h], piece), piece)
            yield pltpu.make_async_copy(
                halo_refs[h].at[r], x_ref.at[r, pl.ds(0, halo), where], sems.at[r, 2 * h]
            )
            yield pltpu.make_async_copy(
                row_refs[r * halves + h], x_ref.at[r, pl.ds(halo, rows), where], sems.at[r, 2 * h + 1]
            )

    @pl.when((tile == 0) & (run == 0))
    def _():
        for r in range(runs):
            for copy in copies(r):
                copy.start()

    @pl.when(run == 0)
    def _():
        proj[:, :, :8, :] = jnp.zeros((3, chans // LANES, 8, LANES), jnp.float32)
        for g in range(groups):
            row = jnp.broadcast_to(fr_ref[g : g + 1, :], (span, 2 * span))
            band[g * span : (g + 1) * span, :] = pltpu.roll(
                row, 0, 1, stride=1, stride_axis=0
            ).astype(band.dtype)

    for r in range(runs):

        @pl.when((tile == 0) & (run == r))
        def _():
            for copy in copies(r):
                copy.wait()

    edges = [0, halo] + list(range(halo + ROW_TILE, total + 1, ROW_TILE))
    for low, high in zip(edges[:-1], edges[1:]):
        if depth % LANES == 0:
            starts = [pl.multiple_of(at_ref[u], LANES) for u in range(len(units))]
            x = jnp.concatenate([x_ref[run, low:high, pl.ds(at, depth)] for at in starts], axis=1)
        else:
            x = x_ref[run, low:high, :]
        for streams in [(0, 1, 2)] if chans == LANES else [(0,), (1,), (2,)]:
            weight = jnp.concatenate(
                [jnp.concatenate([w[q, k, s] for w, q, k in units], axis=0) for s in streams], axis=1
            )
            acc = jnp.dot(x, weight, preferred_element_type=jnp.float32)
            acc = acc.astype(jnp.bfloat16).astype(jnp.float32)
            for n, s in enumerate(streams):
                for h in range(chans // LANES):
                    lane = n * chans + h * LANES
                    proj[s, h, 8 + low : 8 + high, :] = acc[:, lane : lane + LANES]

    def short(s, start, size, h, allowed):
        lanes = slice(h * LANES, (h + 1) * LANES)
        running = proj[s, h, 8 + start : 8 + start + size, :] * sw_ref[s, 0:1, lanes]
        for j in range(1, taps):
            window = proj[s, h, 8 + start - j : 8 + start - j + size, :]
            running = running + jnp.where(allowed[j], window * sw_ref[s, j : j + 1, lanes], 0.0)
        return running

    step = 64
    for r in range(halo - span, total, step):
        pos = pos_ref[0, r : r + step, :]
        allowed = [pos >= j for j in range(taps)]
        for h in range(chans // LANES):
            mixed = short(0, r, step, h, allowed) * short(2, r, step, h, allowed)
            mix[r : r + step, h * LANES : (h + 1) * LANES] = mixed.astype(mix.dtype)

    lag = (
        lax.broadcasted_iota(jnp.int32, (span, 2 * span), 0)
        + span
        - lax.broadcasted_iota(jnp.int32, (span, 2 * span), 1)
    )
    lane_group = lax.broadcasted_iota(jnp.int32, (span, LANES), 1) // width
    for b in range(rows // span):
        first = halo + b * span
        pos = pos_ref[0, first : first + span, :]
        limit = jnp.concatenate([pos] * (2 * span // LANES), axis=1)
        keep = jnp.where(lag <= limit, 1.0, 0.0).astype(band.dtype)
        allowed = [pos >= j for j in range(taps)]
        for h in range(chans // LANES):
            lanes = slice(h * LANES, (h + 1) * LANES)
            some = band[h * per_lanes * span : (h + 1) * per_lanes * span, :]
            some = some.reshape(per_lanes, span, 2 * span) * keep[None]
            full = jnp.dot(
                some.reshape(per_lanes * span, 2 * span),
                mix[first - span : first + span, lanes],
                preferred_element_type=jnp.float32,
            )
            medium = full[:span]
            for g in range(1, per_lanes):
                medium = jnp.where(lane_group == g, full[g * span : (g + 1) * span], medium)
            gated = short(1, first, span, h, allowed) * medium
            done[b * span : (b + 1) * span, lanes] = gated.astype(done.dtype)

    for r in range(runs):

        @pl.when(run == r)
        def _():
            out_refs[r][...] = done[...]


def block(at, rows, halos, weights, sw, fr, pos, span, chans):
    runs, halves = len(rows), len(halos)
    row_count, features = rows[0][0].shape[0], rows[0][0].shape[1] * halves
    total = halos[0].shape[1] + row_count
    taps = sw.shape[1]
    tile = CHAN_TILE if all(n % CHAN_TILE == 0 for n in [chans] + [first for first, _ in weights]) else LANES
    per_tile = tile * fr.shape[0] // chans
    grid = (chans // tile, runs)
    anywhere = pl.BlockSpec(memory_space=pl.ANY)

    def weight_spec(first, w):
        return pl.BlockSpec(w.shape[:4] + (tile,), lambda j, i, at: (0, 0, 0, 0, first // tile + j))

    return pl.pallas_call(
        functools.partial(block_kernel, runs, halves, len(weights)),
        grid_spec=pltpu.PrefetchScalarGridSpec(
            num_scalar_prefetch=1,
            grid=grid,
            in_specs=[weight_spec(first, w) for first, w in weights]
            + [
                pl.BlockSpec((3, taps, tile), lambda j, i, at: (0, 0, j)),
                pl.BlockSpec((per_tile, 2 * span), lambda j, i, at: (j, 0)),
                pl.BlockSpec((1, total, LANES), lambda j, i, at: (i, 0, 0)),
            ]
            + [anywhere] * (runs * halves + halves),
            out_specs=[pl.BlockSpec((row_count, tile), lambda j, i, at: (0, j))] * runs,
            scratch_shapes=[
                pltpu.VMEM((runs, total, features), jnp.bfloat16),
                pltpu.SemaphoreType.DMA((runs, 2 * halves)),
                pltpu.VMEM((3, tile // LANES, 8 + total, LANES), jnp.float32),
                pltpu.VMEM((total, tile), jnp.bfloat16),
                pltpu.VMEM((per_tile * span, 2 * span), jnp.bfloat16),
                pltpu.VMEM((row_count, tile), jnp.bfloat16),
            ],
        ),
        out_shape=[jax.ShapeDtypeStruct((row_count, chans), jnp.bfloat16)] * runs,
        compiler_params=pltpu.CompilerParams(vmem_limit_bytes=56 * 1024 * 1024),
        cost_estimate=pl.CostEstimate(
            flops=4 * runs * total * features * 3 * chans,
            bytes_accessed=2 * (runs * total * features + 3 * features * chans + runs * row_count * chans),
            transcendentals=0,
        ),
    )(at, *[w for _, w in weights], sw, fr, pos, *[half for run in rows for half in run], *halos)


def parameters(short_weight, medium_filter):
    sw = jnp.transpose(short_weight, (1, 0, 2)).astype(jnp.float32)
    span = medium_filter.shape[0]
    fr = jnp.pad(jnp.flip(medium_filter, axis=0).T.astype(jnp.float32), ((0, 0), (1, span - 1)))
    return sw, fr


def flip(array, bit):
    return lax.ppermute(array, "stretch", [(i, i ^ bit) for i in range(lax.axis_size("stretch"))])


def across(array):
    return lax.ppermute(array, "chan", [(0, 1), (1, 0)])


def rows_before(tokens, stretch_id, reach):
    tail = tokens[tokens.shape[0] - reach :]
    sibling = flip(tail, 1)
    second = stretch_id % 2 == 1
    pairs = [(i, i + 2) for i in range(lax.axis_size("stretch") - 2)]
    before = lax.ppermute(jnp.where(second, tail, sibling), "stretch", pairs)
    return jnp.where(second, sibling, before)


def nothing(array):
    return (array[(0,) * array.ndim].astype(jnp.float32) * 0.0).astype(jnp.int32)


def per_device(tokens, in_weight, short_weight, medium_filter, seq_lengths, stretch_slot):
    row_count, piece = tokens.shape
    depth, _, chans = in_weight.shape
    span, taps = medium_filter.shape[0], short_weight.shape[0]
    me = lax.axis_index("stretch")
    devices = lax.axis_size("stretch")
    order = jnp.arange(devices, dtype=jnp.int32)
    reach = -(-(span + taps - 1) // 16) * 16
    sw, fr = parameters(short_weight, medium_filter)
    local = jnp.transpose(in_weight, (1, 0, 2))

    def stretch_at(device):
        return jnp.sum(jnp.where(stretch_slot == device, order, 0))

    def positions(device):
        places = stretch_at(device) * row_count - reach + jnp.arange(reach + row_count, dtype=jnp.int32)
        return jnp.broadcast_to(in_sequence(places, seq_lengths)[:, None], (reach + row_count, LANES))

    if devices != 16 or lax.axis_size("chan") != 2:
        weight = lax.all_gather(local, "stretch", axis=0, tiled=False)
        halo = rows_before(tokens, stretch_at(me), reach)
        halo = lax.all_gather(halo, "chan", axis=1, tiled=True)
        rows = lax.all_gather(tokens, "chan", axis=1, tiled=True)
        at = jnp.concatenate([order * depth, jnp.zeros(1, jnp.int32)])
        return block(at, [[rows]], [halo[None]], [(0, weight[:, None])], sw, fr, positions(me)[None], span, chans)[0]

    side = lax.axis_index("chan")
    kind = (me >> 2) & 1
    half = chans // 2
    own_begin, other_begin = kind * half, (1 - kind) * half
    widths = WIDTHS if sum(WIDTHS) == half else [half]
    begins = [sum(widths[:c]) for c in range(len(widths))]

    halo = rows_before(tokens, stretch_at(me), reach)
    peer_rows = flip(tokens, 4)
    rows_other = across(tokens)
    peer_rows_other = across(peer_rows)
    peer_halo = flip(halo, 4)
    halos = jnp.stack([halo, peer_halo])
    halos_other = across(halos)
    after = {0: [peer_rows, rows_other, halo], 1: [peer_halo, peer_rows_other], 2: [halos_other]}

    planes = [[4 * z + q for q in range(4)] for z in range(devices // 4)]

    def spread(array):
        return lax.all_gather(array, "stretch", axis=0, tiled=False, axis_index_groups=planes)

    own = lax.dynamic_slice_in_dim(local, own_begin, half, 2)
    peers = [
        flip(lax.dynamic_slice_in_dim(local, other_begin + begin, width, 2), 4) for begin, width in zip(begins, widths)
    ]
    for c, peer in enumerate(peers[1:]):
        after[c] = after.get(c, []) + [peer]
    pos = jnp.stack([positions(me), positions(me ^ 4)])
    at = jnp.concatenate(
        [
            jnp.stack([(me // 4 * 4 + q) * depth for q in range(4)]),
            jnp.stack([((me ^ (4 * k)) // 4 * 4 + q) * depth for q in range(4) for k in (1, 2, 3)]),
            jnp.stack([side * piece, (1 - side) * piece]),
        ]
    )
    own_sw = lax.dynamic_slice_in_dim(sw, own_begin, half, 2)
    own_fr = lax.dynamic_slice_in_dim(fr, own_begin * fr.shape[0] // chans, fr.shape[0] // 2, 0)

    gathered, stack = [spread(own[None])], None
    mine, theirs = [], []
    for c, (begin, width) in enumerate(zip(begins, widths)):
        same, peer = own[:, :, begin : begin + width], peers[c]
        if c == 0:
            other = lax.dynamic_slice_in_dim(local, other_begin, width, 2)
            stack = jnp.stack([peer, flip(same, 8), flip(other, 12)])
        else:
            pair = jnp.stack([same, peer]) + nothing(stack).astype(jnp.bfloat16)
            stack = jnp.concatenate([peer[None], flip(pair, 8)])
        waits = sum(nothing(array) for array in after.get(c, []) + [gathered[-1]])
        stack = stack + waits.astype(jnp.bfloat16)
        gathered.append(spread(stack))
        groups = fr.shape[0] * width // chans
        first_group = begin * fr.shape[0] // chans
        out, peer_out = block(
            at,
            [[tokens, rows_other], [peer_rows, peer_rows_other]],
            [halos, halos_other],
            [(begin, gathered[0]), (0, gathered[c + 1])],
            own_sw[:, :, begin : begin + width],
            own_fr[first_group : first_group + groups],
            pos,
            span,
            width,
        )
        mine.append(out)
        theirs.append(flip(peer_out, 4))
        after[c + 3] = [out]
    mine, theirs = jnp.concatenate(mine, axis=1), jnp.concatenate(theirs, axis=1)
    even = kind == 0
    return jnp.concatenate([jnp.where(even, mine, theirs), jnp.where(even, theirs, mine)], axis=1)


def solution(mesh):
    return jax.shard_map(
        per_device,
        mesh=mesh,
        in_specs=(
            P("stretch", "chan"),
            P("stretch", None, "chan"),
            P(None, None, "chan"),
            P(None, "chan"),
            P(),
            P(),
        ),
        out_specs=P("stretch", "chan"),
        check_vma=False,
    )
```

```python
import functools

import jax
import jax.numpy as jnp
from jax import lax
from jax.experimental import pallas as pl
from jax.experimental.pallas import tpu as pltpu
from jax.sharding import PartitionSpec as P

ROW_TILE = 256
CHAN_TILE = 256
LANES = 128
WIDTHS = [256, 256, 256, 256]


def in_sequence(places, seq_lengths):
    seq_ends = jnp.cumsum(seq_lengths)
    starts = seq_ends - seq_lengths
    inside = (places[:, None] >= starts[None, :]) & (places[:, None] < seq_ends[None, :])
    return jnp.sum(jnp.where(inside, places[:, None] - starts[None, :], 0), axis=1)


def block_kernel(runs, halves, parts, at_ref, *refs):
    w_refs, (sw_ref, fr_ref, pos_ref), refs = refs[:parts], refs[parts : parts + 3], refs[parts + 3 :]
    row_refs, halo_refs = refs[: runs * halves], refs[runs * halves : 2 * runs * halves]
    out_refs = refs[2 * runs * halves : 2 * runs * halves + runs]
    x_ref, sems, proj, mix, band, done = refs[2 * runs * halves + runs :]
    total, features = x_ref.shape[1:]
    rows, chans = out_refs[0].shape
    halo = total - rows
    taps = sw_ref.shape[1]
    groups = fr_ref.shape[0]
    span = band.shape[0] // groups
    per_lanes = groups * LANES // chans
    width = LANES // per_lanes
    depth = w_refs[0].shape[3]
    units = [(w, q, k) for w in w_refs for q in range(w.shape[0]) for k in range(w.shape[1])]
    tile, run = pl.program_id(0), pl.program_id(1)

    def copies(r):
        for h in range(halves):
            piece = features // halves
            where = pl.ds(pl.multiple_of(at_ref[len(units) + h], piece), piece)
            yield pltpu.make_async_copy(
                halo_refs[r * halves + h], x_ref.at[r, pl.ds(0, halo), where], sems.at[r, 2 * h]
            )
            yield pltpu.make_async_copy(
                row_refs[r * halves + h], x_ref.at[r, pl.ds(halo, rows), where], sems.at[r, 2 * h + 1]
            )

    @pl.when((tile == 0) & (run == 0))
    def _():
        for r in range(runs):
            for copy in copies(r):
                copy.start()

    @pl.when(run == 0)
    def _():
        proj[:, :, :8, :] = jnp.zeros((3, chans // LANES, 8, LANES), jnp.float32)
        for g in range(groups):
            row = jnp.broadcast_to(fr_ref[g : g + 1, :], (span, 2 * span))
            band[g * span : (g + 1) * span, :] = pltpu.roll(
                row, 0, 1, stride=1, stride_axis=0
            ).astype(band.dtype)

    for r in range(runs):

        @pl.when((tile == 0) & (run == r))
        def _():
            for copy in copies(r):
                copy.wait()

    edges = [0, halo] + list(range(halo + ROW_TILE, total + 1, ROW_TILE))
    for low, high in zip(edges[:-1], edges[1:]):
        if depth % LANES == 0:
            starts = [pl.multiple_of(at_ref[u], LANES) for u in range(len(units))]
            x = jnp.concatenate([x_ref[run, low:high, pl.ds(at, depth)] for at in starts], axis=1)
        else:
            x = x_ref[run, low:high, :]
        for streams in [(0, 1, 2)] if chans == LANES else [(0,), (1,), (2,)]:
            weight = jnp.concatenate(
                [jnp.concatenate([w[q, k, s] for w, q, k in units], axis=0) for s in streams], axis=1
            )
            acc = jnp.dot(x, weight, preferred_element_type=jnp.float32)
            acc = acc.astype(jnp.bfloat16).astype(jnp.float32)
            for n, s in enumerate(streams):
                for h in range(chans // LANES):
                    lane = n * chans + h * LANES
                    proj[s, h, 8 + low : 8 + high, :] = acc[:, lane : lane + LANES]

    def short(s, start, size, h, allowed):
        lanes = slice(h * LANES, (h + 1) * LANES)
        running = proj[s, h, 8 + start : 8 + start + size, :] * sw_ref[s, 0:1, lanes]
        for j in range(1, taps):
            window = proj[s, h, 8 + start - j : 8 + start - j + size, :]
            running = running + jnp.where(allowed[j], window * sw_ref[s, j : j + 1, lanes], 0.0)
        return running

    step = 64
    for r in range(halo - span, total, step):
        pos = pos_ref[0, r : r + step, :]
        allowed = [pos >= j for j in range(taps)]
        for h in range(chans // LANES):
            mixed = short(0, r, step, h, allowed) * short(2, r, step, h, allowed)
            mix[r : r + step, h * LANES : (h + 1) * LANES] = mixed.astype(mix.dtype)

    lag = (
        lax.broadcasted_iota(jnp.int32, (span, 2 * span), 0)
        + span
        - lax.broadcasted_iota(jnp.int32, (span, 2 * span), 1)
    )
    lane_group = lax.broadcasted_iota(jnp.int32, (span, LANES), 1) // width
    for b in range(rows // span):
        first = halo + b * span
        pos = pos_ref[0, first : first + span, :]
        limit = jnp.concatenate([pos] * (2 * span // LANES), axis=1)
        keep = jnp.where(lag <= limit, 1.0, 0.0).astype(band.dtype)
        allowed = [pos >= j for j in range(taps)]
        for h in range(chans // LANES):
            lanes = slice(h * LANES, (h + 1) * LANES)
            some = band[h * per_lanes * span : (h + 1) * per_lanes * span, :]
            some = some.reshape(per_lanes, span, 2 * span) * keep[None]
            full = jnp.dot(
                some.reshape(per_lanes * span, 2 * span),
                mix[first - span : first + span, lanes],
                preferred_element_type=jnp.float32,
            )
            medium = full[:span]
            for g in range(1, per_lanes):
                medium = jnp.where(lane_group == g, full[g * span : (g + 1) * span], medium)
            gated = short(1, first, span, h, allowed) * medium
            done[b * span : (b + 1) * span, lanes] = gated.astype(done.dtype)

    for r in range(runs):

        @pl.when(run == r)
        def _():
            out_refs[r][...] = done[...]


def block(at, rows, halos, weights, sw, fr, pos, span, chans):
    runs, halves = len(rows), len(rows[0])
    row_count, features = rows[0][0].shape[0], rows[0][0].shape[1] * halves
    total = halos[0][0].shape[0] + row_count
    taps = sw.shape[1]
    tile = CHAN_TILE if all(n % CHAN_TILE == 0 for n in [chans] + [first for first, _ in weights]) else LANES
    per_tile = tile * fr.shape[0] // chans
    grid = (chans // tile, runs)
    anywhere = pl.BlockSpec(memory_space=pl.ANY)

    def weight_spec(first, w):
        return pl.BlockSpec(w.shape[:4] + (tile,), lambda j, i, at: (0, 0, 0, 0, first // tile + j))

    return pl.pallas_call(
        functools.partial(block_kernel, runs, halves, len(weights)),
        grid_spec=pltpu.PrefetchScalarGridSpec(
            num_scalar_prefetch=1,
            grid=grid,
            in_specs=[weight_spec(first, w) for first, w in weights]
            + [
                pl.BlockSpec((3, taps, tile), lambda j, i, at: (0, 0, j)),
                pl.BlockSpec((per_tile, 2 * span), lambda j, i, at: (j, 0)),
                pl.BlockSpec((1, total, LANES), lambda j, i, at: (i, 0, 0)),
            ]
            + [anywhere] * (2 * runs * halves),
            out_specs=[pl.BlockSpec((row_count, tile), lambda j, i, at: (0, j))] * runs,
            scratch_shapes=[
                pltpu.VMEM((runs, total, features), jnp.bfloat16),
                pltpu.SemaphoreType.DMA((runs, 2 * halves)),
                pltpu.VMEM((3, tile // LANES, 8 + total, LANES), jnp.float32),
                pltpu.VMEM((total, tile), jnp.bfloat16),
                pltpu.VMEM((per_tile * span, 2 * span), jnp.bfloat16),
                pltpu.VMEM((row_count, tile), jnp.bfloat16),
            ],
        ),
        out_shape=[jax.ShapeDtypeStruct((row_count, chans), jnp.bfloat16)] * runs,
        compiler_params=pltpu.CompilerParams(vmem_limit_bytes=56 * 1024 * 1024),
        cost_estimate=pl.CostEstimate(
            flops=4 * runs * total * features * 3 * chans,
            bytes_accessed=2 * (runs * total * features + 3 * features * chans + runs * row_count * chans),
            transcendentals=0,
        ),
    )(at, *[w for _, w in weights], sw, fr, pos, *[half for run in rows + halos for half in run])


def parameters(short_weight, medium_filter):
    sw = jnp.transpose(short_weight, (1, 0, 2)).astype(jnp.float32)
    span = medium_filter.shape[0]
    fr = jnp.pad(jnp.flip(medium_filter, axis=0).T.astype(jnp.float32), ((0, 0), (1, span - 1)))
    return sw, fr


def flip(array, bit):
    return lax.ppermute(array, "stretch", [(i, i ^ bit) for i in range(lax.axis_size("stretch"))])


def across(array):
    return lax.ppermute(array, "chan", [(0, 1), (1, 0)])


def rows_before(tokens, stretch_id, reach):
    tail = tokens[tokens.shape[0] - reach :]
    sibling = flip(tail, 1)
    second = stretch_id % 2 == 1
    pairs = [(i, i + 2) for i in range(lax.axis_size("stretch") - 2)]
    before = lax.ppermute(jnp.where(second, tail, sibling), "stretch", pairs)
    return jnp.where(second, sibling, before)


def nothing(array):
    return (array[(0,) * array.ndim].astype(jnp.float32) * 0.0).astype(jnp.int32)


def per_device(tokens, in_weight, short_weight, medium_filter, seq_lengths, stretch_slot):
    row_count, piece = tokens.shape
    depth, _, chans = in_weight.shape
    span, taps = medium_filter.shape[0], short_weight.shape[0]
    me = lax.axis_index("stretch")
    devices = lax.axis_size("stretch")
    order = jnp.arange(devices, dtype=jnp.int32)
    reach = -(-(span + taps - 1) // 16) * 16
    sw, fr = parameters(short_weight, medium_filter)
    local = jnp.transpose(in_weight, (1, 0, 2))

    def stretch_at(device):
        return jnp.sum(jnp.where(stretch_slot == device, order, 0))

    def positions(device):
        places = stretch_at(device) * row_count - reach + jnp.arange(reach + row_count, dtype=jnp.int32)
        return jnp.broadcast_to(in_sequence(places, seq_lengths)[:, None], (reach + row_count, LANES))

    if devices != 16 or lax.axis_size("chan") != 2:
        weight = lax.all_gather(local, "stretch", axis=0, tiled=False)
        halo = rows_before(tokens, stretch_at(me), reach)
        halo = lax.all_gather(halo, "chan", axis=1, tiled=True)
        rows = lax.all_gather(tokens, "chan", axis=1, tiled=True)
        at = jnp.concatenate([order * depth, jnp.zeros(1, jnp.int32)])
        return block(at, [[rows]], [[halo]], [(0, weight[:, None])], sw, fr, positions(me)[None], span, chans)[0]

    side = lax.axis_index("chan")
    kind = (me >> 2) & 1
    half = chans // 2
    own_begin, other_begin = kind * half, (1 - kind) * half
    widths = WIDTHS if sum(WIDTHS) == half else [half]
    begins = [sum(widths[:c]) for c in range(len(widths))]

    planes = [[4 * z + q for q in range(4)] for z in range(devices // 4)]

    def spread(array):
        return lax.all_gather(array, "stretch", axis=0, tiled=False, axis_index_groups=planes)

    own = lax.dynamic_slice_in_dim(local, own_begin, half, 2)
    other = lax.dynamic_slice_in_dim(local, other_begin, half, 2)
    peers = flip(other, 4)
    firsts = [peers[:, :, : widths[0]], flip(own[:, :, : widths[0]], 8), flip(other[:, :, : widths[0]], 12)]

    rows_other = across(tokens)
    peer_rows = flip(tokens, 4)
    peer_rows_other = across(peer_rows)
    halo = rows_before(tokens, stretch_at(me), reach)
    halo_other = across(halo)
    peer_halo = flip(halo, 4)
    peer_halo_other = across(peer_halo)
    after = {
        0: [rows_other, halo],
        1: [peer_rows, halo_other],
        2: [peer_rows_other, peer_halo_other],
    }

    pos = jnp.stack([positions(me), positions(me ^ 4)])
    at = jnp.concatenate(
        [
            jnp.stack([(me // 4 * 4 + q) * depth for q in range(4)]),
            jnp.stack([((me ^ (4 * k)) // 4 * 4 + q) * depth for q in range(4) for k in (1, 2, 3)]),
            jnp.stack([side * piece, (1 - side) * piece]),
        ]
    )
    own_sw = lax.dynamic_slice_in_dim(sw, own_begin, half, 2)
    own_fr = lax.dynamic_slice_in_dim(fr, own_begin * fr.shape[0] // chans, fr.shape[0] // 2, 0)

    gathered, stack = [spread(own[None])], None
    mine, theirs = [], []
    for c, (begin, width) in enumerate(zip(begins, widths)):
        if c == 0:
            stack = jnp.stack(firsts)
        else:
            same = own[:, :, begin : begin + width]
            peer = peers[:, :, begin : begin + width]
            pair = jnp.stack([same, peer]) + nothing(stack).astype(jnp.bfloat16)
            stack = jnp.concatenate([peer[None], flip(pair, 8)])
        waits = sum(nothing(array) for array in after.get(c, []) + [gathered[-1]])
        stack = stack + waits.astype(jnp.bfloat16)
        gathered.append(spread(stack))
        groups = fr.shape[0] * width // chans
        first_group = begin * fr.shape[0] // chans
        out, peer_out = block(
            at,
            [[tokens, rows_other], [peer_rows, peer_rows_other]],
            [[halo, halo_other], [peer_halo, peer_halo_other]],
            [(begin, gathered[0]), (0, gathered[c + 1])],
            own_sw[:, :, begin : begin + width],
            own_fr[first_group : first_group + groups],
            pos,
            span,
            width,
        )
        mine.append(out)
        theirs.append(flip(peer_out, 4))
        after[c + 3] = after.get(c + 3, []) + [out]
    mine, theirs = jnp.concatenate(mine, axis=1), jnp.concatenate(theirs, axis=1)
    even = kind == 0
    return jnp.concatenate([jnp.where(even, mine, theirs), jnp.where(even, theirs, mine)], axis=1)


def solution(mesh):
    return jax.shard_map(
        per_device,
        mesh=mesh,
        in_specs=(
            P("stretch", "chan"),
            P("stretch", None, "chan"),
            P(None, None, "chan"),
            P(None, "chan"),
            P(),
            P(),
        ),
        out_specs=P("stretch", "chan"),
        check_vma=False,
    )
```

```python
import functools

import jax
import jax.numpy as jnp
from jax import lax
from jax.experimental import pallas as pl
from jax.experimental.pallas import tpu as pltpu
from jax.sharding import PartitionSpec as P

CHAN_TILE = 256
LANES = 128
WIDTHS = [256, 256, 256, 256]


def in_sequence(places, seq_lengths):
    seq_ends = jnp.cumsum(seq_lengths)
    starts = seq_ends - seq_lengths
    inside = (places[:, None] >= starts[None, :]) & (places[:, None] < seq_ends[None, :])
    return jnp.sum(jnp.where(inside, places[:, None] - starts[None, :], 0), axis=1)


def block_kernel(runs, halves, parts, at_ref, *refs):
    w_refs, (sw_ref, fr_ref, pos_ref), refs = refs[:parts], refs[parts : parts + 3], refs[parts + 3 :]
    row_refs, halo_refs = refs[: runs * halves], refs[runs * halves : 2 * runs * halves]
    out_refs = refs[2 * runs * halves : 2 * runs * halves + runs]
    x_ref, sems, proj, mix, band, done = refs[2 * runs * halves + runs :]
    total, features = x_ref.shape[1:]
    rows, chans = out_refs[0].shape
    halo = total - rows
    taps = sw_ref.shape[1]
    groups = fr_ref.shape[0]
    span = band.shape[0] // groups
    per_lanes = groups * LANES // chans
    width = LANES // per_lanes
    units = [(w, q, k) for w in w_refs for k in range(w.shape[1]) for q in range(w.shape[0])]
    tile, run = pl.program_id(0), pl.program_id(1)

    blocks = at_ref.shape[0] // halves
    piece = features // (halves * blocks)

    def copies(r):
        for h in range(halves):
            for b in range(blocks):
                n = h * blocks + b
                source = pl.ds(b * piece, piece)
                target = pl.ds(pl.multiple_of(at_ref[n], piece), piece)
                halo_from, rows_from = halo_refs[r * halves + h], row_refs[r * halves + h]
                yield pltpu.make_async_copy(
                    halo_from.at[:, source], x_ref.at[r, pl.ds(0, halo), target], sems.at[r, 2 * n]
                )
                yield pltpu.make_async_copy(
                    rows_from.at[:, source], x_ref.at[r, pl.ds(halo, rows), target], sems.at[r, 2 * n + 1]
                )

    @pl.when((tile == 0) & (run == 0))
    def _():
        for r in range(runs):
            for copy in copies(r):
                copy.start()

    @pl.when(run == 0)
    def _():
        proj[:, :, :8, :] = jnp.zeros((3, chans // LANES, 8, LANES), jnp.float32)
        for g in range(groups):
            row = jnp.broadcast_to(fr_ref[g : g + 1, :], (span, 2 * span))
            band[g * span : (g + 1) * span, :] = pltpu.roll(
                row, 0, 1, stride=1, stride_axis=0
            ).astype(band.dtype)

    for r in range(runs):

        @pl.when((tile == 0) & (run == r))
        def _():
            for copy in copies(r):
                copy.wait()

    for streams in [(0, 1, 2)] if chans == LANES else [(0,), (1,), (2,)]:
        weight = jnp.concatenate(
            [jnp.concatenate([w[q, k, s] for w, q, k in units], axis=0) for s in streams], axis=1
        )
        acc = jnp.dot(x_ref[run], weight, preferred_element_type=jnp.float32)
        acc = acc.astype(jnp.bfloat16).astype(jnp.float32)
        for n, s in enumerate(streams):
            for h in range(chans // LANES):
                lane = n * chans + h * LANES
                proj[s, h, 8:, :] = acc[:, lane : lane + LANES]

    def short(s, start, size, h, allowed):
        lanes = slice(h * LANES, (h + 1) * LANES)
        running = proj[s, h, 8 + start : 8 + start + size, :] * sw_ref[s, 0:1, lanes]
        for j in range(1, taps):
            window = proj[s, h, 8 + start - j : 8 + start - j + size, :]
            running = running + jnp.where(allowed[j], window * sw_ref[s, j : j + 1, lanes], 0.0)
        return running

    step = 64
    for r in range(halo - span, total, step):
        pos = pos_ref[0, r : r + step, :]
        allowed = [pos >= j for j in range(taps)]
        for h in range(chans // LANES):
            mixed = short(0, r, step, h, allowed) * short(2, r, step, h, allowed)
            mix[r : r + step, h * LANES : (h + 1) * LANES] = mixed.astype(mix.dtype)

    lag = (
        lax.broadcasted_iota(jnp.int32, (span, 2 * span), 0)
        + span
        - lax.broadcasted_iota(jnp.int32, (span, 2 * span), 1)
    )
    lane_group = lax.broadcasted_iota(jnp.int32, (span, LANES), 1) // width
    for b in range(rows // span):
        first = halo + b * span
        pos = pos_ref[0, first : first + span, :]
        limit = jnp.concatenate([pos] * (2 * span // LANES), axis=1)
        keep = jnp.where(lag <= limit, 1.0, 0.0).astype(band.dtype)
        allowed = [pos >= j for j in range(taps)]
        for h in range(chans // LANES):
            lanes = slice(h * LANES, (h + 1) * LANES)
            some = band[h * per_lanes * span : (h + 1) * per_lanes * span, :]
            some = some.reshape(per_lanes, span, 2 * span) * keep[None]
            full = jnp.dot(
                some.reshape(per_lanes * span, 2 * span),
                mix[first - span : first + span, lanes],
                preferred_element_type=jnp.float32,
            )
            medium = full[:span]
            for g in range(1, per_lanes):
                medium = jnp.where(lane_group == g, full[g * span : (g + 1) * span], medium)
            gated = short(1, first, span, h, allowed) * medium
            done[b * span : (b + 1) * span, lanes] = gated.astype(done.dtype)

    for r in range(runs):

        @pl.when(run == r)
        def _():
            out_refs[r][...] = done[...]


def block(at, rows, halos, weights, sw, fr, pos, span, chans):
    runs, halves = len(rows), len(rows[0])
    row_count, features = rows[0][0].shape[0], rows[0][0].shape[1] * halves
    total = halos[0][0].shape[0] + row_count
    taps = sw.shape[1]
    tile = CHAN_TILE if all(n % CHAN_TILE == 0 for n in [chans] + [first for first, _ in weights]) else LANES
    per_tile = tile * fr.shape[0] // chans
    grid = (chans // tile, runs)
    anywhere = pl.BlockSpec(memory_space=pl.ANY)

    def weight_spec(first, w):
        return pl.BlockSpec(w.shape[:4] + (tile,), lambda j, i, at: (0, 0, 0, 0, first // tile + j))

    return pl.pallas_call(
        functools.partial(block_kernel, runs, halves, len(weights)),
        grid_spec=pltpu.PrefetchScalarGridSpec(
            num_scalar_prefetch=1,
            grid=grid,
            in_specs=[weight_spec(first, w) for first, w in weights]
            + [
                pl.BlockSpec((3, taps, tile), lambda j, i, at: (0, 0, j)),
                pl.BlockSpec((per_tile, 2 * span), lambda j, i, at: (j, 0)),
                pl.BlockSpec((1, total, LANES), lambda j, i, at: (i, 0, 0)),
            ]
            + [anywhere] * (2 * runs * halves),
            out_specs=[pl.BlockSpec((row_count, tile), lambda j, i, at: (0, j))] * runs,
            scratch_shapes=[
                pltpu.VMEM((runs, total, features), jnp.bfloat16),
                pltpu.SemaphoreType.DMA((runs, 2 * at.shape[0])),
                pltpu.VMEM((3, tile // LANES, 8 + total, LANES), jnp.float32),
                pltpu.VMEM((total, tile), jnp.bfloat16),
                pltpu.VMEM((per_tile * span, 2 * span), jnp.bfloat16),
                pltpu.VMEM((row_count, tile), jnp.bfloat16),
            ],
        ),
        out_shape=[jax.ShapeDtypeStruct((row_count, chans), jnp.bfloat16)] * runs,
        compiler_params=pltpu.CompilerParams(vmem_limit_bytes=56 * 1024 * 1024),
        cost_estimate=pl.CostEstimate(
            flops=4 * runs * total * features * 3 * chans,
            bytes_accessed=2 * (runs * total * features + 3 * features * chans + runs * row_count * chans),
            transcendentals=0,
        ),
    )(at, *[w for _, w in weights], sw, fr, pos, *[half for run in rows + halos for half in run])


def parameters(short_weight, medium_filter):
    sw = jnp.transpose(short_weight, (1, 0, 2)).astype(jnp.float32)
    span = medium_filter.shape[0]
    fr = jnp.pad(jnp.flip(medium_filter, axis=0).T.astype(jnp.float32), ((0, 0), (1, span - 1)))
    return sw, fr


def flip(array, bit):
    return lax.ppermute(array, "stretch", [(i, i ^ bit) for i in range(lax.axis_size("stretch"))])


def across(array):
    return lax.ppermute(array, "chan", [(0, 1), (1, 0)])


def rows_before(tokens, stretch_id, reach):
    tail = tokens[tokens.shape[0] - reach :]
    sibling = flip(tail, 1)
    second = stretch_id % 2 == 1
    pairs = [(i, i + 2) for i in range(lax.axis_size("stretch") - 2)]
    before = lax.ppermute(jnp.where(second, tail, sibling), "stretch", pairs)
    return jnp.where(second, sibling, before)


def nothing(array):
    return (array[(0,) * array.ndim].astype(jnp.float32) * 0.0).astype(jnp.int32)


def per_device(tokens, in_weight, short_weight, medium_filter, seq_lengths, stretch_slot):
    row_count, piece = tokens.shape
    depth, _, chans = in_weight.shape
    span, taps = medium_filter.shape[0], short_weight.shape[0]
    me = lax.axis_index("stretch")
    devices = lax.axis_size("stretch")
    order = jnp.arange(devices, dtype=jnp.int32)
    reach = -(-(span + taps - 1) // 16) * 16
    sw, fr = parameters(short_weight, medium_filter)
    local = jnp.transpose(in_weight, (1, 0, 2))

    def stretch_at(device):
        return jnp.sum(jnp.where(stretch_slot == device, order, 0))

    def positions(device):
        places = stretch_at(device) * row_count - reach + jnp.arange(reach + row_count, dtype=jnp.int32)
        return jnp.broadcast_to(in_sequence(places, seq_lengths)[:, None], (reach + row_count, LANES))

    if devices != 16 or lax.axis_size("chan") != 2:
        weight = lax.all_gather(local, "stretch", axis=0, tiled=False)
        halo = rows_before(tokens, stretch_at(me), reach)
        halo = lax.all_gather(halo, "chan", axis=1, tiled=True)
        rows = lax.all_gather(tokens, "chan", axis=1, tiled=True)
        return block(jnp.zeros(1, jnp.int32), [[rows]], [[halo]], [(0, weight[:, None])], sw, fr, positions(me)[None], span, chans)[0]

    side = lax.axis_index("chan")
    kind = (me >> 2) & 1
    half = chans // 2
    own_begin, other_begin = kind * half, (1 - kind) * half
    widths = WIDTHS if sum(WIDTHS) == half else [half]
    begins = [sum(widths[:c]) for c in range(len(widths))]

    planes = [[4 * z + q for q in range(4)] for z in range(devices // 4)]

    def spread(array):
        return lax.all_gather(array, "stretch", axis=0, tiled=False, axis_index_groups=planes)

    own = lax.dynamic_slice_in_dim(local, own_begin, half, 2)
    other = lax.dynamic_slice_in_dim(local, other_begin, half, 2)
    early = widths[0] + widths[1]
    peers = [flip(other[:, :, :early], 4), flip(other[:, :, early:], 4)]
    firsts = [peers[0][:, :, : widths[0]], flip(own[:, :, : widths[0]], 8), flip(other[:, :, : widths[0]], 12)]

    rows_other = across(tokens)
    peer_rows = flip(tokens, 4)
    peer_rows_other = across(peer_rows)
    halo = rows_before(tokens, stretch_at(me), reach)
    halo_other = across(halo)
    peer_halo = flip(halo, 4)
    peer_halo_other = across(peer_halo)
    after = {
        0: [rows_other, peer_rows],
        1: [peer_rows_other, halo, peers[1]],
        2: [halo_other, peer_halo_other],
    }

    pos = jnp.stack([positions(me), positions(me ^ 4)])
    at = jnp.stack([((me >> 2) ^ (2 * part + b)) * 4 * depth for part in (side, 1 - side) for b in range(2)])
    own_sw = lax.dynamic_slice_in_dim(sw, own_begin, half, 2)
    own_fr = lax.dynamic_slice_in_dim(fr, own_begin * fr.shape[0] // chans, fr.shape[0] // 2, 0)

    gathered, stack = [spread(own[None])], None
    mine, theirs = [], []
    for c, (begin, width) in enumerate(zip(begins, widths)):
        if c == 0:
            stack = jnp.stack(firsts)
        else:
            same = own[:, :, begin : begin + width]
            late = begin >= early
            peer = peers[late][:, :, begin - late * early : begin - late * early + width]
            pair = jnp.stack([same, peer]) + nothing(stack).astype(jnp.bfloat16)
            stack = jnp.concatenate([peer[None], flip(pair, 8)])
        waits = sum(nothing(array) for array in after.get(c, []) + [gathered[-1]])
        stack = stack + waits.astype(jnp.bfloat16)
        gathered.append(spread(stack))
        groups = fr.shape[0] * width // chans
        first_group = begin * fr.shape[0] // chans
        out, peer_out = block(
            at,
            [[tokens, rows_other], [peer_rows, peer_rows_other]],
            [[halo, halo_other], [peer_halo, peer_halo_other]],
            [(begin, gathered[0]), (0, gathered[c + 1])],
            own_sw[:, :, begin : begin + width],
            own_fr[first_group : first_group + groups],
            pos,
            span,
            width,
        )
        mine.append(out)
        theirs.append(flip(peer_out, 4))
        after[c + 3] = after.get(c + 3, []) + [out]
    mine, theirs = jnp.concatenate(mine, axis=1), jnp.concatenate(theirs, axis=1)
    even = kind == 0
    return jnp.concatenate([jnp.where(even, mine, theirs), jnp.where(even, theirs, mine)], axis=1)


def solution(mesh):
    return jax.shard_map(
        per_device,
        mesh=mesh,
        in_specs=(
            P("stretch", "chan"),
            P("stretch", None, "chan"),
            P(None, None, "chan"),
            P(None, "chan"),
            P(),
            P(),
        ),
        out_specs=P("stretch", "chan"),
        check_vma=False,
    )
```

```python
import functools

import jax
import jax.numpy as jnp
from jax import lax
from jax.experimental import pallas as pl
from jax.experimental.pallas import tpu as pltpu
from jax.sharding import PartitionSpec as P

ROW_TILE = 256
CHAN_TILE = 256
LANES = 128
WIDTHS = [256, 256, 256, 256]


def in_sequence(places, seq_lengths):
    seq_ends = jnp.cumsum(seq_lengths)
    starts = seq_ends - seq_lengths
    inside = (places[:, None] >= starts[None, :]) & (places[:, None] < seq_ends[None, :])
    return jnp.sum(jnp.where(inside, places[:, None] - starts[None, :], 0), axis=1)


def block_kernel(runs, halves, parts, at_ref, *refs):
    w_refs, (sw_ref, fr_ref, pos_ref), refs = refs[:parts], refs[parts : parts + 3], refs[parts + 3 :]
    row_refs, halo_refs = refs[: runs * halves], refs[runs * halves : 2 * runs * halves]
    out_refs = refs[2 * runs * halves : 2 * runs * halves + runs]
    x_ref, sems, proj, mix, band, done = refs[2 * runs * halves + runs :]
    total, features = x_ref.shape[1:]
    rows, chans = out_refs[0].shape
    halo = total - rows
    taps = sw_ref.shape[1]
    groups = fr_ref.shape[0]
    span = band.shape[0] // groups
    per_lanes = groups * LANES // chans
    width = LANES // per_lanes
    units = [(w, q, k) for w in w_refs for k in range(w.shape[1]) for q in range(w.shape[0])]
    tile, run = pl.program_id(0), pl.program_id(1)

    blocks = at_ref.shape[0] // halves
    piece = features // (halves * blocks)

    def copies(r):
        for h in range(halves):
            for b in range(blocks):
                n = h * blocks + b
                source = pl.ds(b * piece, piece)
                target = pl.ds(pl.multiple_of(at_ref[n], piece), piece)
                halo_from, rows_from = halo_refs[r * halves + h], row_refs[r * halves + h]
                yield pltpu.make_async_copy(
                    halo_from.at[:, source], x_ref.at[r, pl.ds(0, halo), target], sems.at[r, 2 * n]
                )
                yield pltpu.make_async_copy(
                    rows_from.at[:, source], x_ref.at[r, pl.ds(halo, rows), target], sems.at[r, 2 * n + 1]
                )

    @pl.when((tile == 0) & (run == 0))
    def _():
        for r in range(runs):
            for copy in copies(r):
                copy.start()

    @pl.when(run == 0)
    def _():
        proj[:, :, :8, :] = jnp.zeros((3, chans // LANES, 8, LANES), jnp.float32)
        for g in range(groups):
            row = jnp.broadcast_to(fr_ref[g : g + 1, :], (span, 2 * span))
            band[g * span : (g + 1) * span, :] = pltpu.roll(
                row, 0, 1, stride=1, stride_axis=0
            ).astype(band.dtype)

    for r in range(runs):

        @pl.when((tile == 0) & (run == r))
        def _():
            for copy in copies(r):
                copy.wait()

    edges = [0, halo] + list(range(halo + ROW_TILE, total + 1, ROW_TILE))
    for streams in [(0, 1, 2)] if chans == LANES else [(0,), (1,), (2,)]:
        for low, high in zip(edges[:-1], edges[1:]):
            weight = jnp.concatenate(
                [jnp.concatenate([w[q, k, s] for w, q, k in units], axis=0) for s in streams], axis=1
            )
            acc = jnp.dot(x_ref[run, low:high, :], weight, preferred_element_type=jnp.float32)
            acc = acc.astype(jnp.bfloat16).astype(jnp.float32)
            for n, s in enumerate(streams):
                for h in range(chans // LANES):
                    lane = n * chans + h * LANES
                    proj[s, h, 8 + low : 8 + high, :] = acc[:, lane : lane + LANES]

    def short(s, start, size, h, allowed):
        lanes = slice(h * LANES, (h + 1) * LANES)
        running = proj[s, h, 8 + start : 8 + start + size, :] * sw_ref[s, 0:1, lanes]
        for j in range(1, taps):
            window = proj[s, h, 8 + start - j : 8 + start - j + size, :]
            running = running + jnp.where(allowed[j], window * sw_ref[s, j : j + 1, lanes], 0.0)
        return running

    step = 64
    for r in range(halo - span, total, step):
        pos = pos_ref[0, r : r + step, :]
        allowed = [pos >= j for j in range(taps)]
        for h in range(chans // LANES):
            mixed = short(0, r, step, h, allowed) * short(2, r, step, h, allowed)
            mix[r : r + step, h * LANES : (h + 1) * LANES] = mixed.astype(mix.dtype)

    lag = (
        lax.broadcasted_iota(jnp.int32, (span, 2 * span), 0)
        + span
        - lax.broadcasted_iota(jnp.int32, (span, 2 * span), 1)
    )
    lane_group = lax.broadcasted_iota(jnp.int32, (span, LANES), 1) // width
    for b in range(rows // span):
        first = halo + b * span
        pos = pos_ref[0, first : first + span, :]
        limit = jnp.concatenate([pos] * (2 * span // LANES), axis=1)
        keep = jnp.where(lag <= limit, 1.0, 0.0).astype(band.dtype)
        allowed = [pos >= j for j in range(taps)]
        for h in range(chans // LANES):
            lanes = slice(h * LANES, (h + 1) * LANES)
            some = band[h * per_lanes * span : (h + 1) * per_lanes * span, :]
            some = some.reshape(per_lanes, span, 2 * span) * keep[None]
            full = jnp.dot(
                some.reshape(per_lanes * span, 2 * span),
                mix[first - span : first + span, lanes],
                preferred_element_type=jnp.float32,
            )
            medium = full[:span]
            for g in range(1, per_lanes):
                medium = jnp.where(lane_group == g, full[g * span : (g + 1) * span], medium)
            gated = short(1, first, span, h, allowed) * medium
            done[b * span : (b + 1) * span, lanes] = gated.astype(done.dtype)

    for r in range(runs):

        @pl.when(run == r)
        def _():
            out_refs[r][...] = done[...]


def block(at, rows, halos, weights, sw, fr, pos, span, chans):
    runs, halves = len(rows), len(rows[0])
    row_count, features = rows[0][0].shape[0], rows[0][0].shape[1] * halves
    total = halos[0][0].shape[0] + row_count
    taps = sw.shape[1]
    tile = CHAN_TILE if all(n % CHAN_TILE == 0 for n in [chans] + [first for first, _ in weights]) else LANES
    per_tile = tile * fr.shape[0] // chans
    grid = (chans // tile, runs)
    anywhere = pl.BlockSpec(memory_space=pl.ANY)

    def weight_spec(first, w):
        return pl.BlockSpec(w.shape[:4] + (tile,), lambda j, i, at: (0, 0, 0, 0, first // tile + j))

    return pl.pallas_call(
        functools.partial(block_kernel, runs, halves, len(weights)),
        grid_spec=pltpu.PrefetchScalarGridSpec(
            num_scalar_prefetch=1,
            grid=grid,
            in_specs=[weight_spec(first, w) for first, w in weights]
            + [
                pl.BlockSpec((3, taps, tile), lambda j, i, at: (0, 0, j)),
                pl.BlockSpec((per_tile, 2 * span), lambda j, i, at: (j, 0)),
                pl.BlockSpec((1, total, LANES), lambda j, i, at: (i, 0, 0)),
            ]
            + [anywhere] * (2 * runs * halves),
            out_specs=[pl.BlockSpec((row_count, tile), lambda j, i, at: (0, j))] * runs,
            scratch_shapes=[
                pltpu.VMEM((runs, total, features), jnp.bfloat16),
                pltpu.SemaphoreType.DMA((runs, 2 * at.shape[0])),
                pltpu.VMEM((3, tile // LANES, 8 + total, LANES), jnp.float32),
                pltpu.VMEM((total, tile), jnp.bfloat16),
                pltpu.VMEM((per_tile * span, 2 * span), jnp.bfloat16),
                pltpu.VMEM((row_count, tile), jnp.bfloat16),
            ],
        ),
        out_shape=[jax.ShapeDtypeStruct((row_count, chans), jnp.bfloat16)] * runs,
        compiler_params=pltpu.CompilerParams(vmem_limit_bytes=56 * 1024 * 1024),
        cost_estimate=pl.CostEstimate(
            flops=4 * runs * total * features * 3 * chans,
            bytes_accessed=2 * (runs * total * features + 3 * features * chans + runs * row_count * chans),
            transcendentals=0,
        ),
    )(at, *[w for _, w in weights], sw, fr, pos, *[half for run in rows + halos for half in run])


def parameters(short_weight, medium_filter):
    sw = jnp.transpose(short_weight, (1, 0, 2)).astype(jnp.float32)
    span = medium_filter.shape[0]
    fr = jnp.pad(jnp.flip(medium_filter, axis=0).T.astype(jnp.float32), ((0, 0), (1, span - 1)))
    return sw, fr


def flip(array, bit):
    return lax.ppermute(array, "stretch", [(i, i ^ bit) for i in range(lax.axis_size("stretch"))])


def across(array):
    return lax.ppermute(array, "chan", [(0, 1), (1, 0)])


def rows_before(tokens, stretch_id, reach):
    tail = tokens[tokens.shape[0] - reach :]
    sibling = flip(tail, 1)
    second = stretch_id % 2 == 1
    pairs = [(i, i + 2) for i in range(lax.axis_size("stretch") - 2)]
    before = lax.ppermute(jnp.where(second, tail, sibling), "stretch", pairs)
    return jnp.where(second, sibling, before)


def nothing_kernel(*refs):
    pass


def tied(value, *others):
    return pl.pallas_call(
        nothing_kernel,
        in_specs=[pl.BlockSpec(memory_space=pl.ANY)] * (1 + len(others)),
        out_specs=pl.BlockSpec(memory_space=pl.ANY),
        out_shape=jax.ShapeDtypeStruct(value.shape, value.dtype),
        input_output_aliases={0: 0},
        compiler_params=pltpu.CompilerParams(vmem_limit_bytes=56 * 1024 * 1024),
        cost_estimate=pl.CostEstimate(flops=0, bytes_accessed=0, transcendentals=0),
    )(value, *others)


def per_device(tokens, in_weight, short_weight, medium_filter, seq_lengths, stretch_slot):
    row_count, piece = tokens.shape
    depth, _, chans = in_weight.shape
    span, taps = medium_filter.shape[0], short_weight.shape[0]
    me = lax.axis_index("stretch")
    devices = lax.axis_size("stretch")
    order = jnp.arange(devices, dtype=jnp.int32)
    reach = -(-(span + taps - 1) // 16) * 16
    sw, fr = parameters(short_weight, medium_filter)
    local = jnp.transpose(in_weight, (1, 0, 2))

    def stretch_at(device):
        return jnp.sum(jnp.where(stretch_slot == device, order, 0))

    def positions(device):
        places = stretch_at(device) * row_count - reach + jnp.arange(reach + row_count, dtype=jnp.int32)
        return jnp.broadcast_to(in_sequence(places, seq_lengths)[:, None], (reach + row_count, LANES))

    if devices != 16 or lax.axis_size("chan") != 2:
        weight = lax.all_gather(local, "stretch", axis=0, tiled=False)
        halo = rows_before(tokens, stretch_at(me), reach)
        halo = lax.all_gather(halo, "chan", axis=1, tiled=True)
        rows = lax.all_gather(tokens, "chan", axis=1, tiled=True)
        return block(jnp.zeros(1, jnp.int32), [[rows]], [[halo]], [(0, weight[:, None])], sw, fr, positions(me)[None], span, chans)[0]

    side = lax.axis_index("chan")
    kind = (me >> 2) & 1
    half = chans // 2
    own_begin, other_begin = kind * half, (1 - kind) * half
    widths = WIDTHS if sum(WIDTHS) == half else [half]
    begins = [sum(widths[:c]) for c in range(len(widths))]

    planes = [[4 * z + q for q in range(4)] for z in range(devices // 4)]

    def spread(array):
        return lax.all_gather(array, "stretch", axis=0, tiled=False, axis_index_groups=planes)

    own = lax.dynamic_slice_in_dim(local, own_begin, half, 2)
    other = lax.dynamic_slice_in_dim(local, other_begin, half, 2)
    early = widths[0] + widths[1]
    peers = [flip(other[:, :, :early], 4), flip(other[:, :, early:], 4)]
    firsts = [peers[0][:, :, : widths[0]], flip(own[:, :, : widths[0]], 8), flip(other[:, :, : widths[0]], 12)]

    rows_other = across(tokens)
    peer_rows = flip(tokens, 4)
    peer_rows_other = across(peer_rows)
    halo = rows_before(tokens, stretch_at(me), reach)
    halo_other = across(halo)
    peer_halo = flip(halo, 4)
    peer_halo_other = across(peer_halo)
    after = {
        0: [rows_other, peer_rows],
        1: [peer_rows_other, halo, peers[1]],
        2: [halo_other, peer_halo_other],
    }

    pos = jnp.stack([positions(me), positions(me ^ 4)])
    at = jnp.stack([((me >> 2) ^ (2 * part + b)) * 4 * depth for part in (side, 1 - side) for b in range(2)])
    own_sw = lax.dynamic_slice_in_dim(sw, own_begin, half, 2)
    own_fr = lax.dynamic_slice_in_dim(fr, own_begin * fr.shape[0] // chans, fr.shape[0] // 2, 0)

    after[0] += [pos, own_sw, own_fr]
    gathered, stack = [spread(own[None])], None
    mine, theirs = [], []
    for c, (begin, width) in enumerate(zip(begins, widths)):
        if c == 0:
            stack = jnp.stack(firsts)
        else:
            same = own[:, :, begin : begin + width]
            late = begin >= early
            peer = peers[late][:, :, begin - late * early : begin - late * early + width]
            pair = tied(jnp.stack([same, peer]), stack)
            stack = jnp.concatenate([peer[None], flip(pair, 8)])
        stack = tied(stack, gathered[-1], *after.get(c, []))
        gathered.append(spread(stack))
        groups = fr.shape[0] * width // chans
        first_group = begin * fr.shape[0] // chans
        out, peer_out = block(
            at,
            [[tokens, rows_other], [peer_rows, peer_rows_other]],
            [[halo, halo_other], [peer_halo, peer_halo_other]],
            [(begin, gathered[0]), (0, gathered[c + 1])],
            own_sw[:, :, begin : begin + width],
            own_fr[first_group : first_group + groups],
            pos,
            span,
            width,
        )
        mine.append(out)
        theirs.append(flip(peer_out, 4))
        after[c + 3] = after.get(c + 3, []) + [out]
    mine, theirs = jnp.concatenate(mine, axis=1), jnp.concatenate(theirs, axis=1)
    even = kind == 0
    return jnp.concatenate([jnp.where(even, mine, theirs), jnp.where(even, theirs, mine)], axis=1)


def solution(mesh):
    return jax.shard_map(
        per_device,
        mesh=mesh,
        in_specs=(
            P("stretch", "chan"),
            P("stretch", None, "chan"),
            P(None, None, "chan"),
            P(None, "chan"),
            P(),
            P(),
        ),
        out_specs=P("stretch", "chan"),
        check_vma=False,
    )
```

```python
import functools

import jax
import jax.numpy as jnp
from jax import lax
from jax.experimental import pallas as pl
from jax.experimental.pallas import tpu as pltpu
from jax.sharding import PartitionSpec as P

ROW_TILE = 256
CHAN_TILE = 256
LANES = 128
WIDTHS = [256, 256, 384, 128]


def in_sequence(places, seq_lengths):
    seq_ends = jnp.cumsum(seq_lengths)
    starts = seq_ends - seq_lengths
    inside = (places[:, None] >= starts[None, :]) & (places[:, None] < seq_ends[None, :])
    return jnp.sum(jnp.where(inside, places[:, None] - starts[None, :], 0), axis=1)


def block_kernel(runs, halves, parts, at_ref, *refs):
    w_refs, (sw_ref, fr_ref, pos_ref), refs = refs[:parts], refs[parts : parts + 3], refs[parts + 3 :]
    row_refs, halo_refs = refs[: runs * halves], refs[runs * halves : 2 * runs * halves]
    out_refs = refs[2 * runs * halves : 2 * runs * halves + runs]
    x_ref, sems, proj, mix, band, done = refs[2 * runs * halves + runs :]
    total, features = x_ref.shape[1:]
    rows, chans = out_refs[0].shape
    halo = total - rows
    taps = sw_ref.shape[1]
    groups = fr_ref.shape[0]
    span = band.shape[0] // groups
    per_lanes = groups * LANES // chans
    width = LANES // per_lanes
    units = [(w, q, k) for w in w_refs for k in range(w.shape[1]) for q in range(w.shape[0])]
    tile, run = pl.program_id(0), pl.program_id(1)

    blocks = at_ref.shape[0] // halves
    piece = features // (halves * blocks)

    def copies(r):
        for h in range(halves):
            for b in range(blocks):
                n = h * blocks + b
                source = pl.ds(b * piece, piece)
                target = pl.ds(pl.multiple_of(at_ref[n], piece), piece)
                halo_from, rows_from = halo_refs[r * halves + h], row_refs[r * halves + h]
                yield pltpu.make_async_copy(
                    halo_from.at[:, source], x_ref.at[r, pl.ds(0, halo), target], sems.at[r, 2 * n]
                )
                yield pltpu.make_async_copy(
                    rows_from.at[:, source], x_ref.at[r, pl.ds(halo, rows), target], sems.at[r, 2 * n + 1]
                )

    @pl.when((tile == 0) & (run == 0))
    def _():
        for r in range(runs):
            for copy in copies(r):
                copy.start()

    @pl.when(run == 0)
    def _():
        proj[:, :, :8, :] = jnp.zeros((3, chans // LANES, 8, LANES), jnp.float32)
        for g in range(groups):
            row = jnp.broadcast_to(fr_ref[g : g + 1, :], (span, 2 * span))
            band[g * span : (g + 1) * span, :] = pltpu.roll(
                row, 0, 1, stride=1, stride_axis=0
            ).astype(band.dtype)

    for r in range(runs):

        @pl.when((tile == 0) & (run == r))
        def _():
            for copy in copies(r):
                copy.wait()

    edges = [0, halo] + list(range(halo + ROW_TILE, total + 1, ROW_TILE))
    for streams in [(0, 1, 2)] if chans == LANES else [(0,), (1,), (2,)]:
        for low, high in zip(edges[:-1], edges[1:]):
            weight = jnp.concatenate(
                [jnp.concatenate([w[q, k, s] for w, q, k in units], axis=0) for s in streams], axis=1
            )
            acc = jnp.dot(x_ref[run, low:high, :], weight, preferred_element_type=jnp.float32)
            acc = acc.astype(jnp.bfloat16).astype(jnp.float32)
            for n, s in enumerate(streams):
                for h in range(chans // LANES):
                    lane = n * chans + h * LANES
                    proj[s, h, 8 + low : 8 + high, :] = acc[:, lane : lane + LANES]

    def short(s, start, size, h, allowed):
        lanes = slice(h * LANES, (h + 1) * LANES)
        running = proj[s, h, 8 + start : 8 + start + size, :] * sw_ref[s, 0:1, lanes]
        for j in range(1, taps):
            window = proj[s, h, 8 + start - j : 8 + start - j + size, :]
            running = running + jnp.where(allowed[j], window * sw_ref[s, j : j + 1, lanes], 0.0)
        return running

    step = 64
    for r in range(halo - span, total, step):
        pos = pos_ref[0, r : r + step, :]
        allowed = [pos >= j for j in range(taps)]
        for h in range(chans // LANES):
            mixed = short(0, r, step, h, allowed) * short(2, r, step, h, allowed)
            mix[r : r + step, h * LANES : (h + 1) * LANES] = mixed.astype(mix.dtype)

    lag = (
        lax.broadcasted_iota(jnp.int32, (span, 2 * span), 0)
        + span
        - lax.broadcasted_iota(jnp.int32, (span, 2 * span), 1)
    )
    lane_group = lax.broadcasted_iota(jnp.int32, (span, LANES), 1) // width
    for b in range(rows // span):
        first = halo + b * span
        pos = pos_ref[0, first : first + span, :]
        limit = jnp.concatenate([pos] * (2 * span // LANES), axis=1)
        keep = jnp.where(lag <= limit, 1.0, 0.0).astype(band.dtype)
        allowed = [pos >= j for j in range(taps)]
        for h in range(chans // LANES):
            lanes = slice(h * LANES, (h + 1) * LANES)
            some = band[h * per_lanes * span : (h + 1) * per_lanes * span, :]
            some = some.reshape(per_lanes, span, 2 * span) * keep[None]
            full = jnp.dot(
                some.reshape(per_lanes * span, 2 * span),
                mix[first - span : first + span, lanes],
                preferred_element_type=jnp.float32,
            )
            medium = full[:span]
            for g in range(1, per_lanes):
                medium = jnp.where(lane_group == g, full[g * span : (g + 1) * span], medium)
            gated = short(1, first, span, h, allowed) * medium
            done[b * span : (b + 1) * span, lanes] = gated.astype(done.dtype)

    for r in range(runs):

        @pl.when(run == r)
        def _():
            out_refs[r][...] = done[...]


def block(at, rows, halos, weights, sw, fr, pos, span, chans):
    runs, halves = len(rows), len(rows[0])
    row_count, features = rows[0][0].shape[0], rows[0][0].shape[1] * halves
    total = halos[0][0].shape[0] + row_count
    taps = sw.shape[1]
    tile = CHAN_TILE if all(n % CHAN_TILE == 0 for n in [chans] + [first for first, _ in weights]) else LANES
    per_tile = tile * fr.shape[0] // chans
    grid = (chans // tile, runs)
    anywhere = pl.BlockSpec(memory_space=pl.ANY)

    def weight_spec(first, w):
        return pl.BlockSpec(w.shape[:4] + (tile,), lambda j, i, at: (0, 0, 0, 0, first // tile + j))

    return pl.pallas_call(
        functools.partial(block_kernel, runs, halves, len(weights)),
        grid_spec=pltpu.PrefetchScalarGridSpec(
            num_scalar_prefetch=1,
            grid=grid,
            in_specs=[weight_spec(first, w) for first, w in weights]
            + [
                pl.BlockSpec((3, taps, tile), lambda j, i, at: (0, 0, j)),
                pl.BlockSpec((per_tile, 2 * span), lambda j, i, at: (j, 0)),
                pl.BlockSpec((1, total, LANES), lambda j, i, at: (i, 0, 0)),
            ]
            + [anywhere] * (2 * runs * halves),
            out_specs=[pl.BlockSpec((row_count, tile), lambda j, i, at: (0, j))] * runs,
            scratch_shapes=[
                pltpu.VMEM((runs, total, features), jnp.bfloat16),
                pltpu.SemaphoreType.DMA((runs, 2 * at.shape[0])),
                pltpu.VMEM((3, tile // LANES, 8 + total, LANES), jnp.float32),
                pltpu.VMEM((total, tile), jnp.bfloat16),
                pltpu.VMEM((per_tile * span, 2 * span), jnp.bfloat16),
                pltpu.VMEM((row_count, tile), jnp.bfloat16),
            ],
        ),
        out_shape=[jax.ShapeDtypeStruct((row_count, chans), jnp.bfloat16)] * runs,
        compiler_params=pltpu.CompilerParams(vmem_limit_bytes=56 * 1024 * 1024),
        cost_estimate=pl.CostEstimate(
            flops=4 * runs * total * features * 3 * chans,
            bytes_accessed=2 * (runs * total * features + 3 * features * chans + runs * row_count * chans),
            transcendentals=0,
        ),
    )(at, *[w for _, w in weights], sw, fr, pos, *[half for run in rows + halos for half in run])


def parameters(short_weight, medium_filter):
    sw = jnp.transpose(short_weight, (1, 0, 2)).astype(jnp.float32)
    span = medium_filter.shape[0]
    fr = jnp.pad(jnp.flip(medium_filter, axis=0).T.astype(jnp.float32), ((0, 0), (1, span - 1)))
    return sw, fr


def flip(array, bit):
    return lax.ppermute(array, "stretch", [(i, i ^ bit) for i in range(lax.axis_size("stretch"))])


def across(array):
    return lax.ppermute(array, "chan", [(0, 1), (1, 0)])


def rows_before(tokens, stretch_id, reach):
    tail = tokens[tokens.shape[0] - reach :]
    sibling = flip(tail, 1)
    second = stretch_id % 2 == 1
    pairs = [(i, i + 2) for i in range(lax.axis_size("stretch") - 2)]
    before = lax.ppermute(jnp.where(second, tail, sibling), "stretch", pairs)
    return jnp.where(second, sibling, before)


def nothing_kernel(*refs):
    pass


def tied(value, *others):
    return pl.pallas_call(
        nothing_kernel,
        in_specs=[pl.BlockSpec(memory_space=pl.ANY)] * (1 + len(others)),
        out_specs=pl.BlockSpec(memory_space=pl.ANY),
        out_shape=jax.ShapeDtypeStruct(value.shape, value.dtype),
        input_output_aliases={0: 0},
        compiler_params=pltpu.CompilerParams(vmem_limit_bytes=56 * 1024 * 1024),
        cost_estimate=pl.CostEstimate(flops=0, bytes_accessed=0, transcendentals=0),
    )(value, *others)


def per_device(tokens, in_weight, short_weight, medium_filter, seq_lengths, stretch_slot):
    row_count, piece = tokens.shape
    depth, _, chans = in_weight.shape
    span, taps = medium_filter.shape[0], short_weight.shape[0]
    me = lax.axis_index("stretch")
    devices = lax.axis_size("stretch")
    order = jnp.arange(devices, dtype=jnp.int32)
    reach = -(-(span + taps - 1) // 16) * 16
    sw, fr = parameters(short_weight, medium_filter)
    local = jnp.transpose(in_weight, (1, 0, 2))

    def stretch_at(device):
        return jnp.sum(jnp.where(stretch_slot == device, order, 0))

    def positions(device):
        places = stretch_at(device) * row_count - reach + jnp.arange(reach + row_count, dtype=jnp.int32)
        return jnp.broadcast_to(in_sequence(places, seq_lengths)[:, None], (reach + row_count, LANES))

    if devices != 16 or lax.axis_size("chan") != 2 or chans != 2 * sum(WIDTHS):
        weight = lax.all_gather(local, "stretch", axis=0, tiled=False)
        halo = rows_before(tokens, stretch_at(me), reach)
        halo = lax.all_gather(halo, "chan", axis=1, tiled=True)
        rows = lax.all_gather(tokens, "chan", axis=1, tiled=True)
        return block(jnp.zeros(1, jnp.int32), [[rows]], [[halo]], [(0, weight[:, None])], sw, fr, positions(me)[None], span, chans)[0]

    side = lax.axis_index("chan")
    kind = (me >> 2) & 1
    half = chans // 2
    own_begin, other_begin = kind * half, (1 - kind) * half
    widths = WIDTHS
    begins = [sum(widths[:c]) for c in range(len(widths))]

    planes = [[4 * z + q for q in range(4)] for z in range(devices // 4)]

    def spread(array):
        return lax.all_gather(array, "stretch", axis=0, tiled=False, axis_index_groups=planes)

    own = lax.dynamic_slice_in_dim(local, own_begin, half, 2)
    other = lax.dynamic_slice_in_dim(local, other_begin, half, 2)
    early = widths[0] + widths[1]
    peers = [flip(other[:, :, :early], 4), flip(other[:, :, early:], 4)]
    firsts = [peers[0][:, :, : widths[0]], flip(own[:, :, : widths[0]], 8), flip(other[:, :, : widths[0]], 12)]

    rows_other = across(tokens)
    peer_rows = flip(tokens, 4)
    peer_rows_other = across(peer_rows)
    halo = rows_before(tokens, stretch_at(me), reach)
    halo_other = across(halo)
    peer_halo = flip(halo, 4)
    peer_halo_other = across(peer_halo)
    after = {
        0: [rows_other, peer_rows],
        1: [peer_rows_other, halo, peers[1]],
        2: [halo_other, peer_halo_other],
    }

    pos = jnp.stack([positions(me), positions(me ^ 4)])
    at = jnp.stack([((me >> 2) ^ (2 * part + b)) * 4 * depth for part in (side, 1 - side) for b in range(2)])
    own_sw = lax.dynamic_slice_in_dim(sw, own_begin, half, 2)
    own_fr = lax.dynamic_slice_in_dim(fr, own_begin * fr.shape[0] // chans, fr.shape[0] // 2, 0)

    after[0] += [pos, own_sw, own_fr]
    gathered, stack = [spread(own[None])], None
    mine, theirs = [], []

    def convolve(c, scale):
        for start in range(0, widths[c], CHAN_TILE):
            width = min(CHAN_TILE, widths[c] - start)
            first = begins[c] + start
            groups, first_group = (n * fr.shape[0] // chans for n in (width, first))
            out, peer_out = block(
                at,
                [[tokens, rows_other], [peer_rows, peer_rows_other]],
                [[halo, halo_other], [peer_halo, peer_halo_other]],
                [(first, gathered[0]), (start, gathered[c + 1])],
                scale[:, :, first : first + width],
                own_fr[first_group : first_group + groups],
                pos,
                span,
                width,
            )
            mine.append(out)
            theirs.append(flip(peer_out, 4))

    last = len(widths) - 1
    for c, (begin, width) in enumerate(zip(begins, widths)):
        if c == 0:
            stack = jnp.stack(firsts)
        else:
            same = own[:, :, begin : begin + width]
            late = begin >= early
            peer = peers[late][:, :, begin - late * early : begin - late * early + width]
            pair = tied(jnp.stack([same, peer]), stack)
            stack = jnp.concatenate([peer[None], flip(pair, 8)])
        if c == last:
            convolve(0, own_sw)
            convolve(1, tied(own_sw, stack))
            after[c] = after.get(c, []) + mine
        stack = tied(stack, gathered[-1], *after.get(c, []))
        gathered.append(spread(stack))
    for c in range(2, len(widths)):
        convolve(c, own_sw)
    mine, theirs = jnp.concatenate(mine, axis=1), jnp.concatenate(theirs, axis=1)
    even = kind == 0
    return jnp.concatenate([jnp.where(even, mine, theirs), jnp.where(even, theirs, mine)], axis=1)


def solution(mesh):
    return jax.shard_map(
        per_device,
        mesh=mesh,
        in_specs=(
            P("stretch", "chan"),
            P("stretch", None, "chan"),
            P(None, None, "chan"),
            P(None, "chan"),
            P(),
            P(),
        ),
        out_specs=P("stretch", "chan"),
        check_vma=False,
    )
```

```python
import functools

import jax
import jax.numpy as jnp
from jax import lax
from jax.experimental import pallas as pl
from jax.experimental.pallas import tpu as pltpu
from jax.sharding import PartitionSpec as P

ROW_TILE = 256
CHAN_TILE = 256
LANES = 128
WIDTHS = [256, 256, 256, 256]


def in_sequence(places, seq_lengths):
    seq_ends = jnp.cumsum(seq_lengths)
    starts = seq_ends - seq_lengths
    inside = (places[:, None] >= starts[None, :]) & (places[:, None] < seq_ends[None, :])
    return jnp.sum(jnp.where(inside, places[:, None] - starts[None, :], 0), axis=1)


def block_kernel(runs, halves, parts, at_ref, *refs):
    w_refs, (sw_ref, fr_ref, pos_ref), refs = refs[:parts], refs[parts : parts + 3], refs[parts + 3 :]
    row_refs, halo_refs = refs[: runs * halves], refs[runs * halves : 2 * runs * halves]
    out_refs = refs[2 * runs * halves : 2 * runs * halves + runs]
    x_ref, sems, proj, mix, band, done = refs[2 * runs * halves + runs :]
    total, features = x_ref.shape[1:]
    rows, chans = out_refs[0].shape
    halo = total - rows
    taps = sw_ref.shape[1]
    groups = fr_ref.shape[0]
    span = band.shape[0] // groups
    per_lanes = groups * LANES // chans
    width = LANES // per_lanes
    units = [(w, q, k) for w in w_refs for k in range(w.shape[1]) for q in range(w.shape[0])]
    tile, run = pl.program_id(0), pl.program_id(1)

    blocks = at_ref.shape[0] // halves
    piece = features // (halves * blocks)

    def copies(r):
        for h in range(halves):
            for b in range(blocks):
                n = h * blocks + b
                source = pl.ds(b * piece, piece)
                target = pl.ds(pl.multiple_of(at_ref[n], piece), piece)
                halo_from, rows_from = halo_refs[r * halves + h], row_refs[r * halves + h]
                yield pltpu.make_async_copy(
                    halo_from.at[:, source], x_ref.at[r, pl.ds(0, halo), target], sems.at[r, 2 * n]
                )
                yield pltpu.make_async_copy(
                    rows_from.at[:, source], x_ref.at[r, pl.ds(halo, rows), target], sems.at[r, 2 * n + 1]
                )

    @pl.when((tile == 0) & (run == 0))
    def _():
        for r in range(runs):
            for copy in copies(r):
                copy.start()

    @pl.when(run == 0)
    def _():
        proj[:, :, :8, :] = jnp.zeros((3, chans // LANES, 8, LANES), jnp.float32)
        for g in range(groups):
            row = jnp.broadcast_to(fr_ref[g : g + 1, :], (span, 2 * span))
            band[g * span : (g + 1) * span, :] = pltpu.roll(
                row, 0, 1, stride=1, stride_axis=0
            ).astype(band.dtype)

    for r in range(runs):

        @pl.when((tile == 0) & (run == r))
        def _():
            for copy in copies(r):
                copy.wait()

    def project(low, high):
        for streams in [(0, 1, 2)] if chans == LANES else [(0,), (1,), (2,)]:
            weight = jnp.concatenate(
                [jnp.concatenate([w[q, k, s] for w, q, k in units], axis=0) for s in streams], axis=1
            )
            acc = jnp.dot(x_ref[run, low:high, :], weight, preferred_element_type=jnp.float32)
            acc = acc.astype(jnp.bfloat16).astype(jnp.float32)
            for n, s in enumerate(streams):
                for h in range(chans // LANES):
                    lane = n * chans + h * LANES
                    proj[s, h, 8 + low : 8 + high, :] = acc[:, lane : lane + LANES]

    def short(s, start, size, h, allowed):
        lanes = slice(h * LANES, (h + 1) * LANES)
        running = proj[s, h, 8 + start : 8 + start + size, :] * sw_ref[s, 0:1, lanes]
        for j in range(1, taps):
            window = proj[s, h, 8 + start - j : 8 + start - j + size, :]
            running = running + jnp.where(allowed[j], window * sw_ref[s, j : j + 1, lanes], 0.0)
        return running

    step = 64
    lag = (
        lax.broadcasted_iota(jnp.int32, (span, 2 * span), 0)
        + span
        - lax.broadcasted_iota(jnp.int32, (span, 2 * span), 1)
    )
    lane_group = lax.broadcasted_iota(jnp.int32, (span, LANES), 1) // width

    def convolve(low, high):
        for r in range(max(low, halo - span), high, step):
            pos = pos_ref[0, r : r + step, :]
            allowed = [pos >= j for j in range(taps)]
            for h in range(chans // LANES):
                mixed = short(0, r, step, h, allowed) * short(2, r, step, h, allowed)
                mix[r : r + step, h * LANES : (h + 1) * LANES] = mixed.astype(mix.dtype)
        for first in range(max(low, halo), high, span):
            pos = pos_ref[0, first : first + span, :]
            limit = jnp.concatenate([pos] * (2 * span // LANES), axis=1)
            keep = jnp.where(lag <= limit, 1.0, 0.0).astype(band.dtype)
            allowed = [pos >= j for j in range(taps)]
            for h in range(chans // LANES):
                lanes = slice(h * LANES, (h + 1) * LANES)
                some = band[h * per_lanes * span : (h + 1) * per_lanes * span, :]
                some = some.reshape(per_lanes, span, 2 * span) * keep[None]
                full = jnp.dot(
                    some.reshape(per_lanes * span, 2 * span),
                    mix[first - span : first + span, lanes],
                    preferred_element_type=jnp.float32,
                )
                medium = full[:span]
                for g in range(1, per_lanes):
                    medium = jnp.where(lane_group == g, full[g * span : (g + 1) * span], medium)
                gated = short(1, first, span, h, allowed) * medium
                done[first - halo : first - halo + span, lanes] = gated.astype(done.dtype)

    edges = [0, halo] + list(range(halo + ROW_TILE, total + 1, ROW_TILE))
    tiles = list(zip(edges[:-1], edges[1:]))
    project(*tiles[0])
    for before, now in zip(tiles[:-1], tiles[1:]):
        project(*now)
        convolve(*before)
    convolve(*tiles[-1])

    for r in range(runs):

        @pl.when(run == r)
        def _():
            out_refs[r][...] = done[...]


def block(at, rows, halos, weights, sw, fr, pos, span, chans):
    runs, halves = len(rows), len(rows[0])
    row_count, features = rows[0][0].shape[0], rows[0][0].shape[1] * halves
    total = halos[0][0].shape[0] + row_count
    taps = sw.shape[1]
    tile = CHAN_TILE if all(n % CHAN_TILE == 0 for n in [chans] + [first for first, _ in weights]) else LANES
    per_tile = tile * fr.shape[0] // chans
    grid = (chans // tile, runs)
    anywhere = pl.BlockSpec(memory_space=pl.ANY)

    def weight_spec(first, w):
        return pl.BlockSpec(w.shape[:4] + (tile,), lambda j, i, at: (0, 0, 0, 0, first // tile + j))

    return pl.pallas_call(
        functools.partial(block_kernel, runs, halves, len(weights)),
        grid_spec=pltpu.PrefetchScalarGridSpec(
            num_scalar_prefetch=1,
            grid=grid,
            in_specs=[weight_spec(first, w) for first, w in weights]
            + [
                pl.BlockSpec((3, taps, tile), lambda j, i, at: (0, 0, j)),
                pl.BlockSpec((per_tile, 2 * span), lambda j, i, at: (j, 0)),
                pl.BlockSpec((1, total, LANES), lambda j, i, at: (i, 0, 0)),
            ]
            + [anywhere] * (2 * runs * halves),
            out_specs=[pl.BlockSpec((row_count, tile), lambda j, i, at: (0, j))] * runs,
            scratch_shapes=[
                pltpu.VMEM((runs, total, features), jnp.bfloat16),
                pltpu.SemaphoreType.DMA((runs, 2 * at.shape[0])),
                pltpu.VMEM((3, tile // LANES, 8 + total, LANES), jnp.float32),
                pltpu.VMEM((total, tile), jnp.bfloat16),
                pltpu.VMEM((per_tile * span, 2 * span), jnp.bfloat16),
                pltpu.VMEM((row_count, tile), jnp.bfloat16),
            ],
        ),
        out_shape=[jax.ShapeDtypeStruct((row_count, chans), jnp.bfloat16)] * runs,
        compiler_params=pltpu.CompilerParams(vmem_limit_bytes=56 * 1024 * 1024),
        cost_estimate=pl.CostEstimate(
            flops=runs * total * features * chans,
            bytes_accessed=runs * row_count * chans,
            transcendentals=0,
        ),
    )(at, *[w for _, w in weights], sw, fr, pos, *[half for run in rows + halos for half in run])


def parameters(short_weight, medium_filter):
    sw = jnp.transpose(short_weight, (1, 0, 2)).astype(jnp.float32)
    span = medium_filter.shape[0]
    fr = jnp.pad(jnp.flip(medium_filter, axis=0).T.astype(jnp.float32), ((0, 0), (1, span - 1)))
    return sw, fr


def flip(array, bit):
    return lax.ppermute(array, "stretch", [(i, i ^ bit) for i in range(lax.axis_size("stretch"))])


def across(array):
    return lax.ppermute(array, "chan", [(0, 1), (1, 0)])


def rows_before(tokens, stretch_id, reach):
    tail = tokens[tokens.shape[0] - reach :]
    sibling = flip(tail, 1)
    second = stretch_id % 2 == 1
    pairs = [(i, i + 2) for i in range(lax.axis_size("stretch") - 2)]
    before = lax.ppermute(jnp.where(second, tail, sibling), "stretch", pairs)
    return jnp.where(second, sibling, before)


def nothing_kernel(*refs):
    pass


def tied(value, *others):
    return pl.pallas_call(
        nothing_kernel,
        in_specs=[pl.BlockSpec(memory_space=pl.ANY)] * (1 + len(others)),
        out_specs=pl.BlockSpec(memory_space=pl.ANY),
        out_shape=jax.ShapeDtypeStruct(value.shape, value.dtype),
        input_output_aliases={0: 0},
        compiler_params=pltpu.CompilerParams(vmem_limit_bytes=56 * 1024 * 1024),
        cost_estimate=pl.CostEstimate(flops=0, bytes_accessed=0, transcendentals=0),
    )(value, *others)


def per_device(tokens, in_weight, short_weight, medium_filter, seq_lengths, stretch_slot):
    row_count, piece = tokens.shape
    depth, _, chans = in_weight.shape
    span, taps = medium_filter.shape[0], short_weight.shape[0]
    me = lax.axis_index("stretch")
    devices = lax.axis_size("stretch")
    order = jnp.arange(devices, dtype=jnp.int32)
    reach = -(-(span + taps - 1) // 16) * 16
    sw, fr = parameters(short_weight, medium_filter)
    local = jnp.transpose(in_weight, (1, 0, 2))

    def stretch_at(device):
        return jnp.sum(jnp.where(stretch_slot == device, order, 0))

    def positions(device):
        places = stretch_at(device) * row_count - reach + jnp.arange(reach + row_count, dtype=jnp.int32)
        return jnp.broadcast_to(in_sequence(places, seq_lengths)[:, None], (reach + row_count, LANES))

    if devices != 16 or lax.axis_size("chan") != 2 or chans != 2 * sum(WIDTHS):
        weight = lax.all_gather(local, "stretch", axis=0, tiled=False)
        halo = rows_before(tokens, stretch_at(me), reach)
        halo = lax.all_gather(halo, "chan", axis=1, tiled=True)
        rows = lax.all_gather(tokens, "chan", axis=1, tiled=True)
        return block(jnp.zeros(1, jnp.int32), [[rows]], [[halo]], [(0, weight[:, None])], sw, fr, positions(me)[None], span, chans)[0]

    side = lax.axis_index("chan")
    kind = (me >> 2) & 1
    half = chans // 2
    own_begin, other_begin = kind * half, (1 - kind) * half
    widths = WIDTHS
    begins = [sum(widths[:c]) for c in range(len(widths))]

    planes = [[4 * z + q for q in range(4)] for z in range(devices // 4)]

    def spread(array):
        return lax.all_gather(array, "stretch", axis=0, tiled=False, axis_index_groups=planes)

    own = lax.dynamic_slice_in_dim(local, own_begin, half, 2)
    other = lax.dynamic_slice_in_dim(local, other_begin, half, 2)
    early = widths[0] + widths[1]
    peers = [flip(other[:, :, :early], 4), flip(other[:, :, early:], 4)]
    firsts = [peers[0][:, :, : widths[0]], flip(own[:, :, : widths[0]], 8), flip(other[:, :, : widths[0]], 12)]

    rows_other = across(tokens)
    peer_rows = flip(tokens, 4)
    peer_rows_other = across(peer_rows)
    halo = rows_before(tokens, stretch_at(me), reach)
    halo_other = across(halo)
    peer_halo = flip(halo, 4)
    peer_halo_other = across(peer_halo)
    after = {
        0: [rows_other, peer_rows],
        1: [peer_rows_other, halo, peers[1]],
        2: [halo_other, peer_halo_other],
    }

    pos = jnp.stack([positions(me), positions(me ^ 4)])
    at = jnp.stack([((me >> 2) ^ (2 * part + b)) * 4 * depth for part in (side, 1 - side) for b in range(2)])
    own_sw = lax.dynamic_slice_in_dim(sw, own_begin, half, 2)
    own_fr = lax.dynamic_slice_in_dim(fr, own_begin * fr.shape[0] // chans, fr.shape[0] // 2, 0)

    after[0] += [pos, own_sw, own_fr]
    gathered, stack = [spread(own[None])], None
    mine, theirs = [], []

    def convolve(c, scale):
        for start in range(0, widths[c], CHAN_TILE):
            width = min(CHAN_TILE, widths[c] - start)
            first = begins[c] + start
            groups, first_group = (n * fr.shape[0] // chans for n in (width, first))
            out, peer_out = block(
                at,
                [[tokens, rows_other], [peer_rows, peer_rows_other]],
                [[halo, halo_other], [peer_halo, peer_halo_other]],
                [(first, gathered[0]), (start, gathered[c + 1])],
                scale[:, :, first : first + width],
                own_fr[first_group : first_group + groups],
                pos,
                span,
                width,
            )
            mine.append(out)
            theirs.append(flip(peer_out, 4))

    last = len(widths) - 1
    for c, (begin, width) in enumerate(zip(begins, widths)):
        if c == 0:
            stack = jnp.stack(firsts)
        else:
            same = own[:, :, begin : begin + width]
            late = begin >= early
            peer = peers[late][:, :, begin - late * early : begin - late * early + width]
            pair = tied(jnp.stack([same, peer]), stack)
            stack = jnp.concatenate([peer[None], flip(pair, 8)])
        if c == last:
            convolve(0, own_sw)
            convolve(1, own_sw)
            after[c] = after.get(c, []) + mine
        stack = tied(stack, gathered[-1], *after.get(c, []))
        gathered.append(spread(stack))
    for c in range(2, len(widths)):
        convolve(c, own_sw)
    mine, theirs = jnp.concatenate(mine, axis=1), jnp.concatenate(theirs, axis=1)
    even = kind == 0
    return jnp.concatenate([jnp.where(even, mine, theirs), jnp.where(even, theirs, mine)], axis=1)


def solution(mesh):
    return jax.shard_map(
        per_device,
        mesh=mesh,
        in_specs=(
            P("stretch", "chan"),
            P("stretch", None, "chan"),
            P(None, None, "chan"),
            P(None, "chan"),
            P(),
            P(),
        ),
        out_specs=P("stretch", "chan"),
        check_vma=False,
    )
```

```python
import functools

import jax
import jax.numpy as jnp
from jax import lax
from jax.experimental import pallas as pl
from jax.experimental.pallas import tpu as pltpu
from jax.sharding import PartitionSpec as P

ROW_TILE = 256
CHAN_TILE = 256
LANES = 128
WIDTHS = [256, 256, 256, 256]


def in_sequence(places, seq_lengths):
    seq_ends = jnp.cumsum(seq_lengths)
    starts = seq_ends - seq_lengths
    inside = (places[:, None] >= starts[None, :]) & (places[:, None] < seq_ends[None, :])
    return jnp.sum(jnp.where(inside, places[:, None] - starts[None, :], 0), axis=1)


def block_kernel(runs, halves, parts, at_ref, *refs):
    w_refs, (sw_ref, fr_ref, pos_ref), refs = refs[:parts], refs[parts : parts + 3], refs[parts + 3 :]
    row_refs, halo_refs = refs[: runs * halves], refs[runs * halves : 2 * runs * halves]
    out_refs = refs[2 * runs * halves : 2 * runs * halves + runs]
    x_ref, sems, proj, mix, band, done = refs[2 * runs * halves + runs :]
    total, features = x_ref.shape[1:]
    rows, chans = out_refs[0].shape
    halo = total - rows
    taps = sw_ref.shape[1]
    groups = fr_ref.shape[0]
    span = band.shape[0] // groups
    per_lanes = groups * LANES // chans
    width = LANES // per_lanes
    units = [(w, q, k) for w in w_refs for k in range(w.shape[1]) for q in range(w.shape[0])]
    tile, run = pl.program_id(0), pl.program_id(1)

    blocks = at_ref.shape[0] // halves
    piece = features // (halves * blocks)

    def copies(r):
        for h in range(halves):
            for b in range(blocks):
                n = h * blocks + b
                source = pl.ds(b * piece, piece)
                target = pl.ds(pl.multiple_of(at_ref[n], piece), piece)
                halo_from, rows_from = halo_refs[r * halves + h], row_refs[r * halves + h]
                yield pltpu.make_async_copy(
                    halo_from.at[:, source], x_ref.at[r, pl.ds(0, halo), target], sems.at[r, 2 * n]
                )
                yield pltpu.make_async_copy(
                    rows_from.at[:, source], x_ref.at[r, pl.ds(halo, rows), target], sems.at[r, 2 * n + 1]
                )

    @pl.when((tile == 0) & (run == 0))
    def _():
        for r in range(runs):
            for copy in copies(r):
                copy.start()

    @pl.when(run == 0)
    def _():
        proj[:, :, :8, :] = jnp.zeros((3, chans // LANES, 8, LANES), jnp.float32)
        for g in range(groups):
            row = jnp.broadcast_to(fr_ref[g : g + 1, :], (span, 2 * span))
            band[g * span : (g + 1) * span, :] = pltpu.roll(
                row, 0, 1, stride=1, stride_axis=0
            ).astype(band.dtype)

    for r in range(runs):

        @pl.when((tile == 0) & (run == r))
        def _():
            for copy in copies(r):
                copy.wait()

    def project(low, high):
        for streams in [(0, 1, 2)] if chans == LANES else [(0,), (1,), (2,)]:
            weight = jnp.concatenate(
                [jnp.concatenate([w[q, k, s] for w, q, k in units], axis=0) for s in streams], axis=1
            )
            acc = jnp.dot(x_ref[run, low:high, :], weight, preferred_element_type=jnp.float32)
            acc = acc.astype(jnp.bfloat16).astype(jnp.float32)
            for n, s in enumerate(streams):
                for h in range(chans // LANES):
                    lane = n * chans + h * LANES
                    proj[s, h, 8 + low : 8 + high, :] = acc[:, lane : lane + LANES]

    def short(s, start, size, h, allowed):
        lanes = slice(h * LANES, (h + 1) * LANES)
        running = proj[s, h, 8 + start : 8 + start + size, :] * sw_ref[s, 0:1, lanes]
        for j in range(1, taps):
            window = proj[s, h, 8 + start - j : 8 + start - j + size, :]
            running = running + jnp.where(allowed[j], window * sw_ref[s, j : j + 1, lanes], 0.0)
        return running

    step = 64
    lag = (
        lax.broadcasted_iota(jnp.int32, (span, 2 * span), 0)
        + span
        - lax.broadcasted_iota(jnp.int32, (span, 2 * span), 1)
    )
    lane_group = lax.broadcasted_iota(jnp.int32, (span, LANES), 1) // width

    def convolve(low, high):
        for r in range(max(low, halo - span), high, step):
            pos = pos_ref[0, r : r + step, :]
            allowed = [pos >= j for j in range(taps)]
            for h in range(chans // LANES):
                mixed = short(0, r, step, h, allowed) * short(2, r, step, h, allowed)
                mix[r : r + step, h * LANES : (h + 1) * LANES] = mixed.astype(mix.dtype)
        for first in range(max(low, halo), high, span):
            pos = pos_ref[0, first : first + span, :]
            limit = jnp.concatenate([pos] * (2 * span // LANES), axis=1)
            keep = jnp.where(lag <= limit, 1.0, 0.0).astype(band.dtype)
            allowed = [pos >= j for j in range(taps)]
            for h in range(chans // LANES):
                lanes = slice(h * LANES, (h + 1) * LANES)
                some = band[h * per_lanes * span : (h + 1) * per_lanes * span, :]
                some = some.reshape(per_lanes, span, 2 * span) * keep[None]
                full = jnp.dot(
                    some.reshape(per_lanes * span, 2 * span),
                    mix[first - span : first + span, lanes],
                    preferred_element_type=jnp.float32,
                )
                medium = full[:span]
                for g in range(1, per_lanes):
                    medium = jnp.where(lane_group == g, full[g * span : (g + 1) * span], medium)
                gated = short(1, first, span, h, allowed) * medium
                done[first - halo : first - halo + span, lanes] = gated.astype(done.dtype)

    edges = [0, halo] + list(range(halo + ROW_TILE, total + 1, ROW_TILE))
    tiles = list(zip(edges[:-1], edges[1:]))
    project(*tiles[0])
    for before, now in zip(tiles[:-1], tiles[1:]):
        project(*now)
        convolve(*before)
    convolve(*tiles[-1])

    for r in range(runs):

        @pl.when(run == r)
        def _():
            out_refs[r][...] = done[...]


def block(at, rows, halos, weights, sw, fr, pos, span, chans):
    runs, halves = len(rows), len(rows[0])
    row_count, features = rows[0][0].shape[0], rows[0][0].shape[1] * halves
    total = halos[0][0].shape[0] + row_count
    taps = sw.shape[1]
    tile = CHAN_TILE if all(n % CHAN_TILE == 0 for n in [chans] + [first for first, _ in weights]) else LANES
    per_tile = tile * fr.shape[0] // sw.shape[2]
    origin = weights[0][0] // tile
    grid = (chans // tile, runs)
    anywhere = pl.BlockSpec(memory_space=pl.ANY)

    def weight_spec(first, w):
        return pl.BlockSpec(w.shape[:4] + (tile,), lambda j, i, at: (0, 0, 0, 0, first // tile + j))

    return pl.pallas_call(
        functools.partial(block_kernel, runs, halves, len(weights)),
        grid_spec=pltpu.PrefetchScalarGridSpec(
            num_scalar_prefetch=1,
            grid=grid,
            in_specs=[weight_spec(first, w) for first, w in weights]
            + [
                pl.BlockSpec((3, taps, tile), lambda j, i, at: (0, 0, origin + j)),
                pl.BlockSpec((per_tile, 2 * span), lambda j, i, at: (origin + j, 0)),
                pl.BlockSpec((1, total, LANES), lambda j, i, at: (i, 0, 0)),
            ]
            + [anywhere] * (2 * runs * halves),
            out_specs=[pl.BlockSpec((row_count, tile), lambda j, i, at: (0, j))] * runs,
            scratch_shapes=[
                pltpu.VMEM((runs, total, features), jnp.bfloat16),
                pltpu.SemaphoreType.DMA((runs, 2 * at.shape[0])),
                pltpu.VMEM((3, tile // LANES, 8 + total, LANES), jnp.float32),
                pltpu.VMEM((total, tile), jnp.bfloat16),
                pltpu.VMEM((per_tile * span, 2 * span), jnp.bfloat16),
                pltpu.VMEM((row_count, tile), jnp.bfloat16),
            ],
        ),
        out_shape=[jax.ShapeDtypeStruct((row_count, chans), jnp.bfloat16)] * runs,
        compiler_params=pltpu.CompilerParams(vmem_limit_bytes=56 * 1024 * 1024),
        cost_estimate=pl.CostEstimate(
            flops=runs * total * features * chans,
            bytes_accessed=runs * row_count * chans,
            transcendentals=0,
        ),
    )(at, *[w for _, w in weights], sw, fr, pos, *[half for run in rows + halos for half in run])


def parameters(short_weight, medium_filter):
    sw = jnp.transpose(short_weight, (1, 0, 2)).astype(jnp.float32)
    span = medium_filter.shape[0]
    fr = jnp.pad(jnp.flip(medium_filter, axis=0).T.astype(jnp.float32), ((0, 0), (1, span - 1)))
    return sw, fr


def flip(array, bit):
    return lax.ppermute(array, "stretch", [(i, i ^ bit) for i in range(lax.axis_size("stretch"))])


def across(array):
    return lax.ppermute(array, "chan", [(0, 1), (1, 0)])


def rows_before(tokens, stretch_id, reach):
    tail = tokens[tokens.shape[0] - reach :]
    sibling = flip(tail, 1)
    second = stretch_id % 2 == 1
    pairs = [(i, i + 2) for i in range(lax.axis_size("stretch") - 2)]
    before = lax.ppermute(jnp.where(second, tail, sibling), "stretch", pairs)
    return jnp.where(second, sibling, before)


def nothing_kernel(*refs):
    pass


def tied(value, *others):
    return pl.pallas_call(
        nothing_kernel,
        in_specs=[pl.BlockSpec(memory_space=pl.ANY)] * (1 + len(others)),
        out_specs=pl.BlockSpec(memory_space=pl.ANY),
        out_shape=jax.ShapeDtypeStruct(value.shape, value.dtype),
        input_output_aliases={0: 0},
        compiler_params=pltpu.CompilerParams(vmem_limit_bytes=56 * 1024 * 1024),
        cost_estimate=pl.CostEstimate(flops=0, bytes_accessed=0, transcendentals=0),
    )(value, *others)


def per_device(tokens, in_weight, short_weight, medium_filter, seq_lengths, stretch_slot):
    row_count, piece = tokens.shape
    depth, _, chans = in_weight.shape
    span, taps = medium_filter.shape[0], short_weight.shape[0]
    me = lax.axis_index("stretch")
    devices = lax.axis_size("stretch")
    order = jnp.arange(devices, dtype=jnp.int32)
    reach = -(-(span + taps - 1) // 16) * 16
    sw, fr = parameters(short_weight, medium_filter)
    local = jnp.transpose(in_weight, (1, 0, 2))

    def stretch_at(device):
        return jnp.sum(jnp.where(stretch_slot == device, order, 0))

    def positions(device):
        places = stretch_at(device) * row_count - reach + jnp.arange(reach + row_count, dtype=jnp.int32)
        return jnp.broadcast_to(in_sequence(places, seq_lengths)[:, None], (reach + row_count, LANES))

    if devices != 16 or lax.axis_size("chan") != 2 or chans != 2 * sum(WIDTHS):
        weight = lax.all_gather(local, "stretch", axis=0, tiled=False)
        halo = rows_before(tokens, stretch_at(me), reach)
        halo = lax.all_gather(halo, "chan", axis=1, tiled=True)
        rows = lax.all_gather(tokens, "chan", axis=1, tiled=True)
        return block(jnp.zeros(1, jnp.int32), [[rows]], [[halo]], [(0, weight[:, None])], sw, fr, positions(me)[None], span, chans)[0]

    side = lax.axis_index("chan")
    kind = (me >> 2) & 1
    half = chans // 2
    own_begin, other_begin = kind * half, (1 - kind) * half
    widths = WIDTHS
    begins = [sum(widths[:c]) for c in range(len(widths))]

    planes = [[4 * z + q for q in range(4)] for z in range(devices // 4)]

    def spread(array):
        return lax.all_gather(array, "stretch", axis=0, tiled=False, axis_index_groups=planes)

    own = lax.dynamic_slice_in_dim(local, own_begin, half, 2)
    other = lax.dynamic_slice_in_dim(local, other_begin, half, 2)
    early = widths[0] + widths[1]
    peers = [flip(other[:, :, :early], 4), flip(other[:, :, early:], 4)]
    firsts = [peers[0][:, :, : widths[0]], flip(own[:, :, : widths[0]], 8), flip(other[:, :, : widths[0]], 12)]

    rows_other = across(tokens)
    peer_rows = flip(tokens, 4)
    peer_rows_other = across(peer_rows)
    halo = rows_before(tokens, stretch_at(me), reach)
    halo_other = across(halo)
    peer_halo = flip(halo, 4)
    peer_halo_other = across(peer_halo)
    after = {
        0: [rows_other, peer_rows],
        1: [peer_rows_other, halo, peers[1]],
        2: [halo_other, peer_halo_other],
    }

    pos = jnp.stack([positions(me), positions(me ^ 4)])
    at = jnp.stack([((me >> 2) ^ (2 * part + b)) * 4 * depth for part in (side, 1 - side) for b in range(2)])
    own_sw = lax.dynamic_slice_in_dim(sw, own_begin, half, 2)
    own_fr = lax.dynamic_slice_in_dim(fr, own_begin * fr.shape[0] // chans, fr.shape[0] // 2, 0)

    after[0] += [pos, own_sw, own_fr]
    gathered, stack = [spread(own[None])], None
    mine, theirs = [], []

    def convolve(c):
        for start in range(0, widths[c], CHAN_TILE):
            width = min(CHAN_TILE, widths[c] - start)
            first = begins[c] + start
            rows = [[tokens, rows_other], [peer_rows, peer_rows_other]]
            halos = [[halo, halo_other], [peer_halo, peer_halo_other]]
            outs = []
            for low, high in [(1, 2), (0, 1)] if c == len(widths) - 1 else [(0, 2)]:
                outs = [
                    *block(
                        at,
                        rows[low:high],
                        halos[low:high],
                        [(first, gathered[0]), (start, gathered[c + 1])],
                        own_sw,
                        own_fr,
                        pos[low:high],
                        span,
                        width,
                    ),
                    *outs,
                ]
            mine.append(outs[0])
            theirs.append(flip(outs[1], 4))

    last = len(widths) - 1
    for c, (begin, width) in enumerate(zip(begins, widths)):
        if c == 0:
            stack = jnp.stack(firsts)
        else:
            same = own[:, :, begin : begin + width]
            late = begin >= early
            peer = peers[late][:, :, begin - late * early : begin - late * early + width]
            pair = tied(jnp.stack([same, peer]), stack)
            stack = jnp.concatenate([peer[None], flip(pair, 8)])
        if c == last:
            convolve(0)
            convolve(1)
            after[c] = after.get(c, []) + mine
        stack = tied(stack, gathered[-1], *after.get(c, []))
        gathered.append(spread(stack))
    for c in range(2, len(widths)):
        convolve(c)
    mine, theirs = jnp.concatenate(mine, axis=1), jnp.concatenate(theirs, axis=1)
    even = kind == 0
    return jnp.concatenate([jnp.where(even, mine, theirs), jnp.where(even, theirs, mine)], axis=1)


def solution(mesh):
    return jax.shard_map(
        per_device,
        mesh=mesh,
        in_specs=(
            P("stretch", "chan"),
            P("stretch", None, "chan"),
            P(None, None, "chan"),
            P(None, "chan"),
            P(),
            P(),
        ),
        out_specs=P("stretch", "chan"),
        check_vma=False,
    )
```

```python
import functools

import jax
import jax.numpy as jnp
from jax import lax
from jax.experimental import pallas as pl
from jax.experimental.pallas import tpu as pltpu
from jax.sharding import PartitionSpec as P

ROW_TILE = 256
CHAN_TILE = 256
LANES = 128
WIDTHS = [256, 256, 256, 256]


def in_sequence(places, seq_lengths):
    seq_ends = jnp.cumsum(seq_lengths)
    starts = seq_ends - seq_lengths
    inside = (places[:, None] >= starts[None, :]) & (places[:, None] < seq_ends[None, :])
    return jnp.sum(jnp.where(inside, places[:, None] - starts[None, :], 0), axis=1)


def block_kernel(runs, halves, parts, at_ref, *refs):
    w_refs, (sw_ref, fr_ref, pos_ref), refs = refs[:parts], refs[parts : parts + 3], refs[parts + 3 :]
    row_refs, halo_refs = refs[: runs * halves], refs[runs * halves : 2 * runs * halves]
    out_refs = refs[2 * runs * halves : 2 * runs * halves + runs]
    x_ref, sems, proj, mix, band, done = refs[2 * runs * halves + runs :]
    total, features = x_ref.shape[1:]
    rows, chans = out_refs[0].shape
    halo = total - rows
    taps = sw_ref.shape[1]
    groups = fr_ref.shape[0]
    span = band.shape[0] // groups
    per_lanes = groups * LANES // chans
    width = LANES // per_lanes
    units = [(w, q, k) for w in w_refs for k in range(w.shape[1]) for q in range(w.shape[0])]
    tile, run = pl.program_id(0), pl.program_id(1)

    blocks = at_ref.shape[0] // halves
    piece = features // (halves * blocks)

    def copies(r):
        for h in range(halves):
            for b in range(blocks):
                n = h * blocks + b
                source = pl.ds(b * piece, piece)
                target = pl.ds(pl.multiple_of(at_ref[n], piece), piece)
                halo_from, rows_from = halo_refs[r * halves + h], row_refs[r * halves + h]
                yield pltpu.make_async_copy(
                    halo_from.at[:, source], x_ref.at[r, pl.ds(0, halo), target], sems.at[r, 2 * n]
                )
                yield pltpu.make_async_copy(
                    rows_from.at[:, source], x_ref.at[r, pl.ds(halo, rows), target], sems.at[r, 2 * n + 1]
                )

    @pl.when((tile == 0) & (run == 0))
    def _():
        for r in range(runs):
            for copy in copies(r):
                copy.start()

    @pl.when(run == 0)
    def _():
        proj[:, :, :8, :] = jnp.zeros((3, chans // LANES, 8, LANES), jnp.float32)
        for g in range(groups):
            row = jnp.broadcast_to(fr_ref[g : g + 1, :], (span, 2 * span))
            band[g * span : (g + 1) * span, :] = pltpu.roll(
                row, 0, 1, stride=1, stride_axis=0
            ).astype(band.dtype)

    for r in range(runs):

        @pl.when((tile == 0) & (run == r))
        def _():
            for copy in copies(r):
                copy.wait()

    def project(low, high):
        for streams in [(0, 1, 2)] if chans == LANES else [(0,), (1,), (2,)]:
            weight = jnp.concatenate(
                [jnp.concatenate([w[q, k, s] for w, q, k in units], axis=0) for s in streams], axis=1
            )
            acc = jnp.dot(x_ref[run, low:high, :], weight, preferred_element_type=jnp.float32)
            acc = acc.astype(jnp.bfloat16).astype(jnp.float32)
            for n, s in enumerate(streams):
                for h in range(chans // LANES):
                    lane = n * chans + h * LANES
                    proj[s, h, 8 + low : 8 + high, :] = acc[:, lane : lane + LANES]

    def short(s, start, size, h, allowed):
        lanes = slice(h * LANES, (h + 1) * LANES)
        running = proj[s, h, 8 + start : 8 + start + size, :] * sw_ref[s, 0:1, lanes]
        for j in range(1, taps):
            window = proj[s, h, 8 + start - j : 8 + start - j + size, :]
            running = running + jnp.where(allowed[j], window * sw_ref[s, j : j + 1, lanes], 0.0)
        return running

    step = 64
    lag = (
        lax.broadcasted_iota(jnp.int32, (span, 2 * span), 0)
        + span
        - lax.broadcasted_iota(jnp.int32, (span, 2 * span), 1)
    )
    lane_group = lax.broadcasted_iota(jnp.int32, (span, LANES), 1) // width

    def convolve(low, high):
        for r in range(max(low, halo - span), high, step):
            pos = pos_ref[0, r : r + step, :]
            allowed = [pos >= j for j in range(taps)]
            for h in range(chans // LANES):
                mixed = short(0, r, step, h, allowed) * short(2, r, step, h, allowed)
                mix[r : r + step, h * LANES : (h + 1) * LANES] = mixed.astype(mix.dtype)
        for first in range(max(low, halo), high, span):
            pos = pos_ref[0, first : first + span, :]
            limit = jnp.concatenate([pos] * (2 * span // LANES), axis=1)
            keep = jnp.where(lag <= limit, 1.0, 0.0).astype(band.dtype)
            allowed = [pos >= j for j in range(taps)]
            for h in range(chans // LANES):
                lanes = slice(h * LANES, (h + 1) * LANES)
                some = band[h * per_lanes * span : (h + 1) * per_lanes * span, :]
                some = some.reshape(per_lanes, span, 2 * span) * keep[None]
                full = jnp.dot(
                    some.reshape(per_lanes * span, 2 * span),
                    mix[first - span : first + span, lanes],
                    preferred_element_type=jnp.float32,
                )
                medium = full[:span]
                for g in range(1, per_lanes):
                    medium = jnp.where(lane_group == g, full[g * span : (g + 1) * span], medium)
                gated = short(1, first, span, h, allowed) * medium
                done[first - halo : first - halo + span, lanes] = gated.astype(done.dtype)

    edges = [0, halo] + list(range(halo + ROW_TILE, total + 1, ROW_TILE))
    tiles = list(zip(edges[:-1], edges[1:]))
    project(*tiles[0])
    for before, now in zip(tiles[:-1], tiles[1:]):
        project(*now)
        convolve(*before)
    convolve(*tiles[-1])

    for r in range(runs):

        @pl.when(run == r)
        def _():
            out_refs[r][...] = done[...]


def block(at, rows, halos, weights, sw, fr, pos, span, chans):
    runs, halves = len(rows), len(rows[0])
    row_count, features = rows[0][0].shape[0], rows[0][0].shape[1] * halves
    total = halos[0][0].shape[0] + row_count
    taps = sw.shape[1]
    tile = CHAN_TILE if all(n % CHAN_TILE == 0 for n in [chans] + [first for first, _ in weights]) else LANES
    per_tile = tile * fr.shape[0] // sw.shape[2]
    origin = weights[0][0] // tile
    grid = (chans // tile, runs)
    anywhere = pl.BlockSpec(memory_space=pl.ANY)

    def weight_spec(first, w):
        return pl.BlockSpec(w.shape[:4] + (tile,), lambda j, i, at: (0, 0, 0, 0, first // tile + j))

    return pl.pallas_call(
        functools.partial(block_kernel, runs, halves, len(weights)),
        grid_spec=pltpu.PrefetchScalarGridSpec(
            num_scalar_prefetch=1,
            grid=grid,
            in_specs=[weight_spec(first, w) for first, w in weights]
            + [
                pl.BlockSpec((3, taps, tile), lambda j, i, at: (0, 0, origin + j)),
                pl.BlockSpec((per_tile, 2 * span), lambda j, i, at: (origin + j, 0)),
                pl.BlockSpec((1, total, LANES), lambda j, i, at: (i, 0, 0)),
            ]
            + [anywhere] * (2 * runs * halves),
            out_specs=[pl.BlockSpec((row_count, tile), lambda j, i, at: (0, j))] * runs,
            scratch_shapes=[
                pltpu.VMEM((runs, total, features), jnp.bfloat16),
                pltpu.SemaphoreType.DMA((runs, 2 * at.shape[0])),
                pltpu.VMEM((3, tile // LANES, 8 + total, LANES), jnp.float32),
                pltpu.VMEM((total, tile), jnp.bfloat16),
                pltpu.VMEM((per_tile * span, 2 * span), jnp.bfloat16),
                pltpu.VMEM((row_count, tile), jnp.bfloat16),
            ],
        ),
        out_shape=[jax.ShapeDtypeStruct((row_count, chans), jnp.bfloat16)] * runs,
        compiler_params=pltpu.CompilerParams(vmem_limit_bytes=56 * 1024 * 1024),
        cost_estimate=pl.CostEstimate(
            flops=runs * total * features * chans,
            bytes_accessed=runs * row_count * chans,
            transcendentals=0,
        ),
    )(at, *[w for _, w in weights], sw, fr, pos, *[half for run in rows + halos for half in run])


def parameters(short_weight, medium_filter):
    sw = jnp.transpose(short_weight, (1, 0, 2)).astype(jnp.float32)
    span = medium_filter.shape[0]
    fr = jnp.pad(jnp.flip(medium_filter, axis=0).T.astype(jnp.float32), ((0, 0), (1, span - 1)))
    return sw, fr


def flip(array, bit):
    return lax.ppermute(array, "stretch", [(i, i ^ bit) for i in range(lax.axis_size("stretch"))])


def across(array):
    return lax.ppermute(array, "chan", [(0, 1), (1, 0)])


def rows_before(tokens, stretch_id, reach):
    tail = tokens[tokens.shape[0] - reach :]
    sibling = flip(tail, 1)
    second = stretch_id % 2 == 1
    pairs = [(i, i + 2) for i in range(lax.axis_size("stretch") - 2)]
    before = lax.ppermute(jnp.where(second, tail, sibling), "stretch", pairs)
    return jnp.where(second, sibling, before)


def nothing_kernel(*refs):
    pass


def tied(value, *others):
    return pl.pallas_call(
        nothing_kernel,
        in_specs=[pl.BlockSpec(memory_space=pl.ANY)] * (1 + len(others)),
        out_specs=pl.BlockSpec(memory_space=pl.ANY),
        out_shape=jax.ShapeDtypeStruct(value.shape, value.dtype),
        input_output_aliases={0: 0},
        compiler_params=pltpu.CompilerParams(vmem_limit_bytes=56 * 1024 * 1024),
        cost_estimate=pl.CostEstimate(flops=0, bytes_accessed=0, transcendentals=0),
    )(value, *others)


def per_device(tokens, in_weight, short_weight, medium_filter, seq_lengths, stretch_slot):
    row_count, piece = tokens.shape
    depth, _, chans = in_weight.shape
    span, taps = medium_filter.shape[0], short_weight.shape[0]
    me = lax.axis_index("stretch")
    devices = lax.axis_size("stretch")
    order = jnp.arange(devices, dtype=jnp.int32)
    reach = -(-(span + taps - 1) // 16) * 16
    sw, fr = parameters(short_weight, medium_filter)
    local = jnp.transpose(in_weight, (1, 0, 2))

    def stretch_at(device):
        return jnp.sum(jnp.where(stretch_slot == device, order, 0))

    def positions(device):
        places = stretch_at(device) * row_count - reach + jnp.arange(reach + row_count, dtype=jnp.int32)
        return jnp.broadcast_to(in_sequence(places, seq_lengths)[:, None], (reach + row_count, LANES))

    if devices != 16 or lax.axis_size("chan") != 2 or chans != 2 * sum(WIDTHS):
        weight = lax.all_gather(local, "stretch", axis=0, tiled=False)
        halo = rows_before(tokens, stretch_at(me), reach)
        halo = lax.all_gather(halo, "chan", axis=1, tiled=True)
        rows = lax.all_gather(tokens, "chan", axis=1, tiled=True)
        return block(jnp.zeros(1, jnp.int32), [[rows]], [[halo]], [(0, weight[:, None])], sw, fr, positions(me)[None], span, chans)[0]

    side = lax.axis_index("chan")
    kind = (me >> 2) & 1
    half = chans // 2
    own_begin, other_begin = kind * half, (1 - kind) * half
    widths = WIDTHS
    begins = [sum(widths[:c]) for c in range(len(widths))]

    planes = [[4 * z + q for q in range(4)] for z in range(devices // 4)]

    def spread(array):
        return lax.all_gather(array, "stretch", axis=0, tiled=False, axis_index_groups=planes)

    own = lax.dynamic_slice_in_dim(local, own_begin, half, 2)
    other = lax.dynamic_slice_in_dim(local, other_begin, half, 2)
    early = widths[0] + widths[1]
    peers = [flip(other[:, :, :early], 4), flip(other[:, :, early:], 4)]
    firsts = [peers[0][:, :, : widths[0]], flip(own[:, :, : widths[0]], 8), flip(other[:, :, : widths[0]], 12)]

    rows_other = across(tokens)
    peer_rows = flip(tokens, 4)
    peer_rows_other = across(peer_rows)
    halo = rows_before(tokens, stretch_at(me), reach)
    halo_other = across(halo)
    peer_halo = flip(halo, 4)
    peer_halo_other = across(peer_halo)
    after = {
        0: [rows_other, peer_rows],
        1: [peer_rows_other, halo, peers[1]],
        2: [halo_other, peer_halo_other],
    }

    pos = jnp.stack([positions(me), positions(me ^ 4)])
    at = jnp.stack([((me >> 2) ^ (2 * part + b)) * 4 * depth for part in (side, 1 - side) for b in range(2)])
    own_sw = lax.dynamic_slice_in_dim(sw, own_begin, half, 2)
    own_fr = lax.dynamic_slice_in_dim(fr, own_begin * fr.shape[0] // chans, fr.shape[0] // 2, 0)

    after[0] += [pos, own_sw, own_fr]
    gathered, stack = [spread(own[None])], None
    mine, theirs = [], []

    def convolve(c):
        for start in range(0, widths[c], CHAN_TILE):
            width = min(CHAN_TILE, widths[c] - start)
            first = begins[c] + start
            rows = [[tokens, rows_other], [peer_rows, peer_rows_other]]
            halos = [[halo, halo_other], [peer_halo, peer_halo_other]]
            out, peer_out = block(
                at, rows, halos, [(first, gathered[0]), (start, gathered[c + 1])], own_sw, own_fr, pos, span, width
            )
            mine.append(out)
            theirs.append(flip(peer_out, 4))

    last = len(widths) - 1
    for c, (begin, width) in enumerate(zip(begins, widths)):
        if c == 0:
            stack = jnp.stack(firsts)
        else:
            same = own[:, :, begin : begin + width]
            late = begin >= early
            peer = peers[late][:, :, begin - late * early : begin - late * early + width]
            pair = tied(jnp.stack([same, peer]), stack)
            stack = jnp.concatenate([peer[None], flip(pair, 8)])
        if c == last:
            convolve(0)
            convolve(1)
            after[c] = after.get(c, []) + mine
        stack = tied(stack, gathered[-1], *after.get(c, []))
        gathered.append(spread(stack))
    for c in range(2, len(widths)):
        convolve(c)
    mine, theirs = jnp.concatenate(mine, axis=1), jnp.concatenate(theirs, axis=1)
    even = kind == 0
    return jnp.concatenate([jnp.where(even, mine, theirs), jnp.where(even, theirs, mine)], axis=1)


def solution(mesh):
    return jax.shard_map(
        per_device,
        mesh=mesh,
        in_specs=(
            P("stretch", "chan"),
            P("stretch", None, "chan"),
            P(None, None, "chan"),
            P(None, "chan"),
            P(),
            P(),
        ),
        out_specs=P("stretch", "chan"),
        check_vma=False,
    )
```
